32 devices in a mesh: ctx: 4 (over z), tp: 4 (over x, core), dp: 2 (over y).
Axes of the slice: x: 2, y: 2, z: 4, core: 2. Of those that a mesh axis runs over, the one named last changes fastest.
Arguments:
- queries: bfloat16 [2, 768, 8192], P('dp', 'ctx', 'tp'), may hold values from -6 to 6
- keys: bfloat16 [2, 768, 8192], P('dp', 'ctx', 'tp'), may hold values from -6 to 6
- values: bfloat16 [2, 768, 8192], P('dp', 'ctx', 'tp'), may hold values from -6 to 6
- out_grad: bfloat16 [2, 768, 8192], P('dp', ('ctx', 'tp')), may hold values from -6 to 6
- filters: float32 [512, 128], P('tp'), may hold values from -0.5 to 0.5
Outputs:
- query_grad: bfloat16 [2, 768, 8192], P('dp', 'ctx', 'tp')
- key_grad: bfloat16 [2, 768, 8192], P('dp', 'ctx', 'tp')
- value_grad: bfloat16 [2, 768, 8192], P('dp', 'ctx', 'tp')
- filter_grad: float32 [512, 128], P('tp')
The draws below stay inside these ranges and needn't reach their ends.
All inputs are finite; a program needn't handle non-finite values.
Results may differ from the reference program's by a relative error of at most 0.006.
Values may be sent and summed in bfloat16 or wider, within the bound.
No kernel may reach another device: no remote copies, remote signals or barrier semaphores. Data moves between devices by JAX's collectives and lax.ppermute only.
A program may use at most 64 MiB of HBM per device.

```python
import math
import jax
import jax.numpy as jnp
from jax import lax

D = 8192
TAPS = 128
GROUP_CH = 16
GROUPS = 512
SEQ = 768
BATCH = 2


def steps_of(rng, dims, cuts, low, high):
    gain, own = 1.0, jax.random.fold_in(rng, 6)
    for dim, parts in cuts:
        draws = jnp.exp(jax.random.uniform(jax.random.fold_in(own, dim), (parts,), jnp.float32, low / len(cuts), high / len(cuts)))
        gain = gain * jnp.repeat(draws, dims[dim] // parts).reshape([-1 if axis == dim else 1 for axis in range(len(dims))])
    return gain


def centred(rng, extent, deviation, bound, shards=(), kind=jnp.bfloat16):
    values = jax.random.normal(rng, extent, jnp.float32) * deviation
    if len(shards) > 0:
        values = steps_of(rng, extent, shards, -0.22, 0.18) * values
    return jnp.clip(values, min=-bound, max=bound).astype(kind)


def setup_inputs(seed: int = 0) -> dict:
    key_list = jax.random.split(jax.random.key(seed), 6)
    queries = centred(key_list[0], (BATCH, SEQ, D), 1.0, 6.0, ((0, 2), (1, 4), (2, 4)))
    keys = centred(key_list[1], (BATCH, SEQ, D), 1.0, 6.0, ((0, 2), (1, 4), (2, 4)))
    values = centred(key_list[2], (BATCH, SEQ, D), 1.0, 6.0, ((0, 2), (1, 4), (2, 4)))
    out_grad = centred(key_list[3], (BATCH, SEQ, D), 1.0, 6.0, ((0, 2), (1, 16)))
    filters = centred(key_list[4], (GROUPS, TAPS), TAPS ** -0.5, 0.5, ((0, 4),), jnp.float32)
    return dict(queries=queries, keys=keys, values=values, out_grad=out_grad, filters=filters)


def rounded(array):
    return lax.optimization_barrier(array.astype(jnp.bfloat16)).astype(jnp.float32)

def reference(queries, keys, values, out_grad, filters):
    batches, length, channels = queries.shape
    tap_count = filters.shape[1]
    block_width = 128
    block_count = channels // block_width
    fft_size = 2 * length
    coeffs = rounded(filters)
    per_channel = jnp.repeat(coeffs, GROUP_CH, axis=0)

    def one_block(position):
        begin_col = position * block_width

        def take(array):
            return lax.dynamic_slice_in_dim(array, begin_col, block_width, 2).astype(jnp.float32)
        query_part = take(queries)
        key_part = take(keys)
        value_part = take(values)
        grad_part = take(out_grad)
        tap_part = lax.dynamic_slice_in_dim(per_channel, begin_col, block_width, 0)
        products = rounded(key_part * value_part)
        grad_mix = rounded(grad_part * query_part)
        filter_freq = jnp.fft.rfft(tap_part.T, n=fft_size, axis=0)
        product_freq = jnp.fft.rfft(products, n=fft_size, axis=1)
        grad_freq = jnp.fft.rfft(grad_mix, n=fft_size, axis=1)
        mixed = jnp.fft.irfft(product_freq * filter_freq, n=fft_size, axis=1)[:, :length]
        back = jnp.fft.irfft(grad_freq * jnp.conj(filter_freq), n=fft_size, axis=1)[:, :length]
        lagged = jnp.fft.irfft(grad_freq * jnp.conj(product_freq), n=fft_size, axis=1)[:, :tap_count]
        return ((grad_part * mixed).astype(jnp.bfloat16), (back * value_part).astype(jnp.bfloat16), (back * key_part).astype(jnp.bfloat16), lax.optimization_barrier(jnp.sum(lagged, axis=0)))
    query_blocks, key_blocks, value_blocks, lag_blocks = lax.map(one_block, jnp.arange(block_count, dtype=jnp.int32))

    def assemble(stacked):
        return jnp.transpose(stacked, (1, 2, 0, 3)).reshape(batches, length, channels)
    per_chan_grad = jnp.transpose(lag_blocks, (0, 2, 1)).reshape(channels, tap_count)
    grouped = per_chan_grad.reshape(channels // GROUP_CH, GROUP_CH, tap_count).sum(axis=1)
    scale = 1.0 / math.sqrt(batches * length * GROUP_CH)
    return (assemble(query_blocks), assemble(key_blocks), assemble(value_blocks), grouped * scale)
```

```python
import functools
import math

import jax
import jax.numpy as jnp
from jax import lax
from jax.experimental import pallas as pl
from jax.experimental.pallas import tpu as pltpu
from jax.sharding import PartitionSpec as P

LANES = 128
BLOCK = 32


def widen(value):
    return value.astype(jnp.float32)


def product(left, right):
    return (widen(left) * widen(right)).astype(jnp.bfloat16)


def passed_along(value, axis, steps):
    count = lax.axis_size(axis)
    first, last = (max(0, -steps), min(count, count - steps))
    return lax.ppermute(value, axis, [(source, source + steps) for source in range(first, last)])


def peer(index, step, count):
    if count & (count - 1) == 0:
        return index ^ step
    return (index + step) % count


def sender(index, step, count):
    if count & (count - 1) == 0:
        return index ^ step
    return (index - step + count) % count


def exchanged(rows, axis):
    count = lax.axis_size(axis)
    here = lax.axis_index(axis)
    height = rows.shape[0]
    width = rows.shape[1] // count
    own = lax.dynamic_slice_in_dim(rows, here * width, width, 1)
    parts = []
    for step in range(1, count):
        part = lax.dynamic_slice_in_dim(rows, peer(here, step, count) * width, width, 1)
        pairs = [(index, peer(index, step, count)) for index in range(count)]
        parts.append((sender(here, step, count), lax.ppermute(part, axis, pairs)))
    result = jnp.zeros((height * count, width), rows.dtype)
    result = lax.dynamic_update_slice_in_dim(result, own, here * height, 0)
    for source, part in parts:
        result = lax.dynamic_update_slice_in_dim(result, part, source * height, 0)
    return result


def summed(value, axis):
    count = lax.axis_size(axis)
    if count & (count - 1):
        return lax.psum(value, axis)
    if count <= 4:
        steps = range(1, count)
        parts = [
            lax.ppermute(value, axis, [(index, index ^ step) for index in range(count)])
            for step in steps
        ]
        for part in parts:
            value = value + part
        return value
    step = 1
    while step < count:
        value = value + lax.ppermute(value, axis, [(i, i ^ step) for i in range(count)])
        step *= 2
    return value


def windows(rows, blocks, height):
    return jnp.concatenate([rows[BLOCK * b : BLOCK * b + height] for b in range(blocks)], axis=1)


def bands(base, count, width):
    rows = []
    for group in range(count):
        row = jnp.broadcast_to(base[group : group + 1, :], (BLOCK, base.shape[1]))
        row = pltpu.roll(row, 0, 1, stride=1, stride_axis=0)
        rows.append(row[:, :width].astype(jnp.bfloat16))
    return jnp.concatenate(rows, axis=0)


def convolved(base, window, blocks, taps, group_width):
    count = LANES // group_width
    every = jnp.dot(
        bands(base, count, taps + BLOCK),
        windows(window, blocks, taps + BLOCK),
        preferred_element_type=jnp.float32,
    )
    lane_group = lax.broadcasted_iota(jnp.int32, (BLOCK, LANES), 1) // group_width
    outs = []
    for b in range(blocks):
        columns = slice(b * LANES, (b + 1) * LANES)
        out = every[:BLOCK, columns]
        for group in range(1, count):
            out = jnp.where(
                lane_group == group, every[group * BLOCK : (group + 1) * BLOCK, columns], out
            )
        outs.append(out)
    return jnp.concatenate(outs, axis=0)


def scores_kernel(taps, group_width, q_ref, og_ref, k_ref, v_ref, early_ref, out_ref):
    blocks = k_ref.shape[0] // BLOCK
    count = LANES // group_width
    down = lax.broadcasted_iota(jnp.int32, (BLOCK, BLOCK), 0)
    across = lax.broadcasted_iota(jnp.int32, (BLOCK, BLOCK), 1)
    reverse = (down + across == BLOCK - 1).astype(jnp.bfloat16)
    lane = lax.broadcasted_iota(jnp.int32, (BLOCK, blocks * LANES), 1)
    lane_group = (lane % LANES) // group_width
    for tile in range(k_ref.shape[1] // LANES):
        c = slice(tile * LANES, (tile + 1) * LANES)
        grad_mix = product(og_ref[:, c], q_ref[:, c])
        window = jnp.concatenate([early_ref[:, c], product(k_ref[:, c], v_ref[:, c])], axis=0)
        own = windows(grad_mix, blocks, BLOCK)
        own = jnp.dot(reverse, own, preferred_element_type=jnp.float32).astype(jnp.bfloat16)
        split = [jnp.where(lane_group == g, own, jnp.zeros_like(own)) for g in range(count)]
        scores = lax.dot_general(
            jnp.concatenate(split, axis=0),
            windows(window, blocks, taps + BLOCK),
            (((1,), (1,)), ((), ())),
            preferred_element_type=jnp.float32,
        )
        spare = jnp.zeros((scores.shape[0], 2 * taps - scores.shape[1]), jnp.float32)
        scores = jnp.concatenate([scores, spare], axis=1)
        for g in range(count):
            part = scores[g * BLOCK : (g + 1) * BLOCK]
            part = pltpu.roll(part, taps - BLOCK, 1, stride=1, stride_axis=0)[:, taps:]
            row = tile * count + g
            out_ref[row : row + 1, :] = jnp.sum(part, axis=0, keepdims=True)


def mixed_kernel(taps, group_width, k_ref, v_ref, early_ref, base_ref, og_ref, out_ref):
    blocks = k_ref.shape[0] // BLOCK
    count = LANES // group_width
    for tile in range(k_ref.shape[1] // LANES):
        c = slice(tile * LANES, (tile + 1) * LANES)
        window = jnp.concatenate([early_ref[:, c], product(k_ref[:, c], v_ref[:, c])], axis=0)
        base = base_ref[tile * count : (tile + 1) * count]
        mixed = convolved(base, window, blocks, taps, group_width)
        out_ref[:, c] = (widen(og_ref[:, c]) * mixed).astype(jnp.bfloat16)


def back_kernel(
    taps, group_width, q_ref, og_ref, late_ref, k_ref, v_ref, base_ref, kg_ref, vg_ref
):
    blocks = k_ref.shape[0] // BLOCK
    count = LANES // group_width
    for tile in range(k_ref.shape[1] // LANES):
        c = slice(tile * LANES, (tile + 1) * LANES)
        window = jnp.concatenate([product(og_ref[:, c], q_ref[:, c]), late_ref[:, c]], axis=0)
        base = base_ref[tile * count : (tile + 1) * count]
        back = convolved(base, window, blocks, taps, group_width)
        kg_ref[:, c] = (back * widen(v_ref[:, c])).astype(jnp.bfloat16)
        vg_ref[:, c] = (back * widen(k_ref[:, c])).astype(jnp.bfloat16)


def call(kernel, name, args, bases, outs, taps, group_width):
    channels = args[0].shape[1]
    wide = math.gcd(channels, 8 * LANES)
    groups = wide // group_width

    def by_column(height):
        return pl.BlockSpec((height, wide), lambda i: (0, i))

    def by_group(width):
        return pl.BlockSpec((groups, width), lambda i: (i, 0))


    return pl.pallas_call(
        functools.partial(kernel, taps, group_width),
        grid=(channels // wide,),
        in_specs=[by_group(a.shape[1]) if a.dtype == jnp.float32 else by_column(a.shape[0]) for a in args],
        out_specs=[by_group(o.shape[1]) if o.dtype == jnp.float32 else by_column(o.shape[0]) for o in outs],
        out_shape=outs,
        name=name,
        cost_estimate=pl.CostEstimate(flops=4_000_000_000, bytes_accessed=3_000_000, transcendentals=0),
        compiler_params=pltpu.CompilerParams(vmem_limit_bytes=48 * 1024 * 1024),
    )(*args)


def local(queries, keys, values, out_grad, filters):
    q, k, v = queries[0], keys[0], values[0]
    rows, channels = q.shape
    groups, taps = filters.shape
    group_width = channels // groups
    coeffs = widen(filters.astype(jnp.bfloat16))
    zeros = jnp.zeros_like(coeffs)
    causal = jnp.concatenate([zeros[:, :1], jnp.flip(coeffs, 1), zeros[:, 1:]], axis=1)
    adjoint = jnp.concatenate([coeffs, zeros], axis=1)
    grad = exchanged(out_grad[0], "tp")
    early = passed_along(product(k[rows - taps :], v[rows - taps :]), "ctx", 1)
    late = passed_along(product(grad[:taps], q[:taps]), "ctx", -1)
    wide = jax.ShapeDtypeStruct((rows, channels), jnp.bfloat16)
    small = jax.ShapeDtypeStruct((groups, taps), jnp.float32)
    (lags,) = call(scores_kernel, "lag_scores", (q, grad, k, v, early), (), [small], taps, group_width)
    lags = summed(summed(lags, "dp"), "ctx")
    (query_grad,) = call(mixed_kernel, "causal", (k, v, early, causal, grad), (), [wide], taps, group_width)
    key_grad, value_grad = call(
        back_kernel, "adjoint", (q, grad, late, k, v, adjoint), (), [wide, wide], taps, group_width
    )
    scale = 1.0 / math.sqrt(lax.axis_size("dp") * lax.axis_size("ctx") * rows * group_width)
    return (query_grad[None], key_grad[None], value_grad[None], jnp.flip(lags, 1) * scale)


def solution(mesh):
    in_specs = (
        P("dp", "ctx", "tp"),
        P("dp", "ctx", "tp"),
        P("dp", "ctx", "tp"),
        P("dp", ("ctx", "tp"), None),
        P("tp", None),
    )
    out_specs = (P("dp", "ctx", "tp"), P("dp", "ctx", "tp"), P("dp", "ctx", "tp"), P("tp", None))
    return jax.shard_map(local, mesh=mesh, in_specs=in_specs, out_specs=out_specs, check_vma=False)
```

```python
import functools
import math

import jax
import jax.numpy as jnp
from jax import lax
from jax.experimental import pallas as pl
from jax.experimental.pallas import tpu as pltpu
from jax.sharding import PartitionSpec as P

LANES = 128
BLOCK = 32
STEP = 4 * LANES
VMEM = pl.BlockSpec(memory_space=pltpu.VMEM)
ANYWHERE = pl.BlockSpec(memory_space=pl.ANY)
SCALAR = pl.BlockSpec(memory_space=pltpu.SMEM)


def in_hbm(value):
    return pltpu.with_memory_space_constraint(value, pltpu.HBM)


def widen(value):
    return value.astype(jnp.float32)


def product(left, right):
    return (widen(left) * widen(right)).astype(jnp.bfloat16)


def passed_along(value, axis, steps):
    count = lax.axis_size(axis)
    first, last = (max(0, -steps), min(count, count - steps))
    return lax.ppermute(value, axis, [(source, source + steps) for source in range(first, last)])


def partner(index, step, count):
    if count & (count - 1) == 0:
        return index ^ step
    return (index - step + count) % count


def target(index, step, count):
    if count & (count - 1) == 0:
        return index ^ step
    return (index + step) % count


def exchanged(parts, axis):
    count = lax.axis_size(axis)
    brought = []
    for step, part in enumerate(parts, 1):
        pairs = [(index, target(index, step, count)) for index in range(count)]
        brought.append(lax.ppermute(part, axis, pairs))
    return brought


def add_kernel(left_ref, right_ref, out_ref):
    out_ref[...] = left_ref[...] + right_ref[...]


def summed(value, axis, after=None):
    count = lax.axis_size(axis)
    if count & (count - 1):
        return lax.psum(value, axis)

    def brought(step):
        return lax.ppermute(value, axis, [(index, index ^ step) for index in range(count)])

    if count == 4:
        parts = [value] + [brought(step) for step in range(1, count)]
        if after is not None:
            parts, after = lax.optimization_barrier((parts, after))
        return (parts[0] + parts[1]) + (parts[2] + parts[3])
    step = 1
    while step < count:
        part = brought(step)
        if after is not None:
            part, after = lax.optimization_barrier((part, after))
        value = pl.pallas_call(
            add_kernel,
            in_specs=[VMEM] * 2,
            out_specs=VMEM,
            out_shape=jax.ShapeDtypeStruct(value.shape, value.dtype),
            name="add",
            compiler_params=pltpu.CompilerParams(vmem_limit_bytes=LIMIT * 1024 * 1024),
        )(value, part)
        step *= 2
    return value


def windows(rows, blocks, height):
    return jnp.concatenate([rows[BLOCK * b : BLOCK * b + height] for b in range(blocks)], axis=1)


def bands(base, count, width):
    rows = []
    for group in range(count):
        row = jnp.broadcast_to(base[group : group + 1, :], (BLOCK, base.shape[1]))
        row = pltpu.roll(row, 0, 1, stride=1, stride_axis=0)
        rows.append(row[:, :width].astype(jnp.bfloat16))
    return jnp.concatenate(rows, axis=0)


def convolved(base, window, blocks, taps, group_width):
    count = LANES // group_width
    every = jnp.dot(
        bands(base, count, taps + BLOCK),
        windows(window, blocks, taps + BLOCK),
        preferred_element_type=jnp.float32,
    )
    lane_group = lax.broadcasted_iota(jnp.int32, (BLOCK, LANES), 1) // group_width
    outs = []
    for b in range(blocks):
        columns = slice(b * LANES, (b + 1) * LANES)
        out = every[:BLOCK, columns]
        for group in range(1, count):
            out = jnp.where(
                lane_group == group, every[group * BLOCK : (group + 1) * BLOCK, columns], out
            )
        outs.append(out)
    return jnp.concatenate(outs, axis=0)


def tiles(channels, group_width):
    count = LANES // group_width
    for tile in range(channels // LANES):
        yield slice(tile * LANES, (tile + 1) * LANES), slice(tile * count, (tile + 1) * count)


def send_out(stage_ref, out_ref, sem, c):
    if c.stop % STEP == 0 or c.stop == stage_ref.shape[1]:
        begin = (c.stop - 1) // STEP * STEP
        columns = pl.ds(begin, c.stop - begin)
        copy = pltpu.make_async_copy(
            stage_ref.at[:, columns], out_ref.at[:, columns], sem.at[begin // STEP]
        )
        copy.start()
        return [copy]
    return []


def pack_kernel(count, grad_ref, k_ref, v_ref, *refs):
    parts, (tail_ref, k_stage, v_stage, stage, part_sem, tail_sem) = refs[:-6], refs[-6:]
    here = lax.axis_index("tp")
    height = k_stage.shape[0]
    width = parts[0].shape[1]
    below = pl.ds(k_ref.shape[0] - height, height)
    tails = [
        pltpu.make_async_copy(ref.at[below], into, tail_sem.at[n])
        for n, (ref, into) in enumerate([(k_ref, k_stage), (v_ref, v_stage)])
    ]
    cuts = []
    for n, part in enumerate(parts):
        place = target(here, n + 1, count) * width
        columns = pl.ds(pl.multiple_of(place, width), width)
        cuts.append(pltpu.make_async_copy(grad_ref.at[:, columns], part, part_sem.at[n]))
    for copy in tails + cuts:
        copy.start()
    for copy in tails:
        copy.wait()
    stage[...] = product(k_stage[...], v_stage[...])
    out = pltpu.make_async_copy(stage, tail_ref, tail_sem.at[0])
    out.start()
    for copy in [out] + cuts:
        copy.wait()


def gather_kernel(count, grad_ref, q_ref, *refs):
    parts, refs = refs[: count - 1], refs[count - 1 :]
    og_refs, (head_ref, q_stage, own_sem, q_sem) = refs[:HALVES], refs[HALVES:]
    height, width = parts[0].shape
    piece = width // HALVES
    here = lax.axis_index("tp")

    def rows_of(step):
        return pl.ds(pl.multiple_of(partner(here, step, count) * height, height), height)

    copies = [pltpu.make_async_copy(q_ref.at[pl.ds(0, q_stage.shape[0])], q_stage, q_sem)]
    for half, og_ref in enumerate(og_refs):
        columns = pl.ds(pl.multiple_of(here * width + half * piece, piece), piece)
        own = pltpu.make_async_copy(
            grad_ref.at[:, columns], og_ref.at[rows_of(0)], own_sem.at[half]
        )
        copies.append(own)
    for copy in copies:
        copy.start()
    for half, og_ref in enumerate(og_refs):
        for step, part in enumerate(parts, 1):
            og_ref[rows_of(step), :] = part[:, half * piece : (half + 1) * piece]
    for copy in copies:
        copy.wait()
    for half, og_ref in enumerate(og_refs):
        c = slice(half * piece, (half + 1) * piece)
        head_ref[:, c] = product(og_ref[: q_stage.shape[0], :], q_stage[:, c])


def columns_of(refs, c):
    width = refs[0].shape[1]
    half = c.start // width
    return refs[half][:, c.start - half * width : c.stop - half * width]


def scores_kernel(taps, group_width, q_ref, *refs):
    og_refs, (k_ref, v_ref, early_ref, out_ref) = refs[:HALVES], refs[HALVES:]
    blocks = k_ref.shape[0] // BLOCK
    count = LANES // group_width
    upward = 7 - lax.broadcasted_iota(jnp.int32, (8, LANES), 0)
    lane = lax.broadcasted_iota(jnp.int32, (BLOCK, blocks * LANES), 1)
    lane_group = (lane % LANES) // group_width
    for c, rows in tiles(k_ref.shape[1], group_width):
        grad_mix = widen(columns_of(og_refs, c)) * widen(q_ref[:, c])
        turned = []
        for b in range(blocks):
            for end in range((b + 1) * BLOCK, b * BLOCK, -8):
                eight = grad_mix[end - 8 : end]
                turned.append(jnp.take_along_axis(eight, upward, axis=0, mode="promise_in_bounds"))
        own = windows(jnp.concatenate(turned, axis=0).astype(jnp.bfloat16), blocks, BLOCK)
        window = jnp.concatenate([early_ref[:, c], product(k_ref[:, c], v_ref[:, c])], axis=0)
        split = [jnp.where(lane_group == g, own, jnp.zeros_like(own)) for g in range(count)]
        scores = lax.dot_general(
            jnp.concatenate(split, axis=0),
            windows(window, blocks, taps + BLOCK),
            (((1,), (1,)), ((), ())),
            preferred_element_type=jnp.float32,
        )
        spare = jnp.zeros((scores.shape[0], 2 * taps - scores.shape[1]), jnp.float32)
        scores = jnp.concatenate([scores, spare], axis=1)
        sums = []
        for g in range(count):
            part = scores[g * BLOCK : (g + 1) * BLOCK]
            part = pltpu.roll(part, taps - BLOCK, 1, stride=1, stride_axis=0)[:, taps:]
            sums.append(jnp.sum(part, axis=0, keepdims=True))
        out_ref[rows, :] = jnp.concatenate(sums, axis=0)


def mixed_kernel(taps, group_width, k_ref, v_ref, early_ref, filter_ref, *refs):
    og_refs, (out_ref, stage_ref, sem) = refs[:HALVES], refs[HALVES:]
    blocks = k_ref.shape[0] // BLOCK
    tap = lax.broadcasted_iota(jnp.int32, (taps, 2 * taps), 0)
    place = lax.broadcasted_iota(jnp.int32, (taps, 2 * taps), 1)
    turn = (tap + place == taps).astype(jnp.bfloat16)
    base = jnp.dot(filter_ref[...].astype(jnp.bfloat16), turn, preferred_element_type=jnp.float32)
    copies = []
    for c, rows in tiles(k_ref.shape[1], group_width):
        window = jnp.concatenate([early_ref[:, c], product(k_ref[:, c], v_ref[:, c])], axis=0)
        mixed = convolved(base[rows], window, blocks, taps, group_width)
        stage_ref[:, c] = (widen(columns_of(og_refs, c)) * mixed).astype(jnp.bfloat16)
        copies += send_out(stage_ref, out_ref, sem, c)
    for copy in copies:
        copy.wait()


def back_kernel(taps, group_width, q_ref, k_ref, v_ref, filter_ref, *refs):
    og_refs, refs = refs[:HALVES], refs[HALVES:]
    late_ref, kg_ref, vg_ref, k_stage, v_stage, k_sem, v_sem = refs
    blocks = k_ref.shape[0] // BLOCK
    coeffs = widen(filter_ref[...].astype(jnp.bfloat16))
    base = jnp.concatenate([coeffs, jnp.zeros_like(coeffs)], axis=1)
    copies = []
    for c, rows in tiles(k_ref.shape[1], group_width):
        grad_mix = product(columns_of(og_refs, c), q_ref[:, c])
        window = jnp.concatenate([grad_mix, late_ref[:, c]], axis=0)
        back = convolved(base[rows], window, blocks, taps, group_width)
        k_stage[:, c] = (back * widen(v_ref[:, c])).astype(jnp.bfloat16)
        v_stage[:, c] = (back * widen(k_ref[:, c])).astype(jnp.bfloat16)
        copies += send_out(k_stage, kg_ref, k_sem, c) + send_out(v_stage, vg_ref, v_sem, c)
    for copy in copies:
        copy.wait()


def call(kernel, name, args, outs, staged, cost):
    steps = -(-outs[0].shape[-1] // STEP)
    stages = [pltpu.VMEM(o.shape, o.dtype) for o in outs] + [pltpu.SemaphoreType.DMA((steps,)) for _ in outs]
    return pl.pallas_call(
        kernel,
        in_specs=[SCALAR if a.dtype == jnp.int32 else VMEM for a in args],
        out_specs=[ANYWHERE if staged else VMEM for _ in outs],
        out_shape=outs,
        scratch_shapes=stages if staged else [],
        name=name,
        cost_estimate=pl.CostEstimate(flops=cost, bytes_accessed=1000, transcendentals=0),
        compiler_params=pltpu.CompilerParams(vmem_limit_bytes=LIMIT * 1024 * 1024),
    )(*args)


def local(queries, keys, values, out_grad, filters):
    q, k, v = queries[0], keys[0], values[0]
    rows, channels = q.shape
    groups, taps = filters.shape
    group_width = channels // groups
    wide = jax.ShapeDtypeStruct((rows, channels), jnp.bfloat16)
    edge = jax.ShapeDtypeStruct((taps, channels), jnp.bfloat16)
    small = jax.ShapeDtypeStruct((groups, taps), jnp.float32)
    half = jax.ShapeDtypeStruct((rows, channels // HALVES), jnp.bfloat16)
    count = lax.axis_size("tp")
    height = rows // count
    piece = jax.ShapeDtypeStruct((height, channels), jnp.bfloat16)
    *parts, tail = pl.pallas_call(
        functools.partial(pack_kernel, count),
        in_specs=[ANYWHERE] * 3,
        out_specs=[ANYWHERE] * count,
        out_shape=[piece] * (count - 1) + [edge],
        scratch_shapes=[pltpu.VMEM(edge.shape, edge.dtype)] * 3
        + [pltpu.SemaphoreType.DMA((count - 1,)), pltpu.SemaphoreType.DMA((2,))],
        name="pack",
        compiler_params=pltpu.CompilerParams(vmem_limit_bytes=LIMIT * 1024 * 1024),
    )(*[in_hbm(a) for a in (out_grad[0], k, v)])
    early = passed_along(tail, "ctx", 1)
    parts = exchanged(parts, "tp")
    if height % 16 == 0:
        *grads, head = pl.pallas_call(
            functools.partial(gather_kernel, count),
            in_specs=[ANYWHERE] * 2 + [VMEM] * (count - 1),
            out_specs=[VMEM] * (HALVES + 1),
            out_shape=[half] * HALVES + [edge],
            scratch_shapes=[pltpu.VMEM(edge.shape, edge.dtype)]
            + [pltpu.SemaphoreType.DMA((HALVES,)), pltpu.SemaphoreType.DMA],
            name="gather",
            compiler_params=pltpu.CompilerParams(vmem_limit_bytes=LIMIT * 1024 * 1024),
        )(in_hbm(out_grad[0]), q, *parts)
    else:
        here = lax.axis_index("tp")
        own = lax.dynamic_slice_in_dim(out_grad[0], here * channels, channels, 1)
        grad = jnp.zeros(wide.shape, wide.dtype)
        for step, part in enumerate([own] + parts):
            place = partner(here, step, count)
            grad = lax.dynamic_update_slice_in_dim(grad, part, place * height, 0)
        head = product(grad[:taps], q[:taps])
        grads = jnp.split(grad, HALVES, axis=1)
    late = passed_along(head, "ctx", -1)
    work = functools.partial
    (lags,) = call(
        work(scores_kernel, taps, group_width), "lag_scores", (q, *grads, k, v, early), [small], False, COST
    )
    (query_grad,) = call(
        work(mixed_kernel, taps, group_width), "causal", (k, v, early, filters, *grads), [wide], True, COST
    )
    lags = summed(lags, "dp", query_grad)
    key_grad, value_grad = call(
        work(back_kernel, taps, group_width), "adjoint", (q, k, v, filters, *grads, late), [wide, wide], True, COST
    )
    lags = summed(lags, "ctx", key_grad)
    scale = 1.0 / math.sqrt(lax.axis_size("dp") * lax.axis_size("ctx") * rows * group_width)
    return (query_grad[None], key_grad[None], value_grad[None], jnp.flip(lags, 1) * scale)


COST = 100_000_000
HALVES = 1
LIMIT = 8


def solution(mesh):
    in_specs = (
        P("dp", "ctx", "tp"),
        P("dp", "ctx", "tp"),
        P("dp", "ctx", "tp"),
        P("dp", ("ctx", "tp"), None),
        P("tp", None),
    )
    out_specs = (P("dp", "ctx", "tp"), P("dp", "ctx", "tp"), P("dp", "ctx", "tp"), P("tp", None))
    return jax.shard_map(local, mesh=mesh, in_specs=in_specs, out_specs=out_specs, check_vma=False)
```

```python
import functools
import math

import jax
import jax.numpy as jnp
from jax import lax
from jax.experimental import pallas as pl
from jax.experimental.pallas import tpu as pltpu
from jax.sharding import PartitionSpec as P

LANES = 128
BLOCK = 32
STEP = 4 * LANES
VMEM = pl.BlockSpec(memory_space=pltpu.VMEM)
ANYWHERE = pl.BlockSpec(memory_space=pl.ANY)
SCALAR = pl.BlockSpec(memory_space=pltpu.SMEM)


def in_hbm(value):
    return pltpu.with_memory_space_constraint(value, pltpu.HBM)


def widen(value):
    return value.astype(jnp.float32)


def product(left, right):
    return (widen(left) * widen(right)).astype(jnp.bfloat16)


def passed_along(value, axis, steps):
    count = lax.axis_size(axis)
    first, last = (max(0, -steps), min(count, count - steps))
    return lax.ppermute(value, axis, [(source, source + steps) for source in range(first, last)])


def partner(index, step, count):
    if count & (count - 1) == 0:
        return index ^ step
    return (index - step + count) % count


def target(index, step, count):
    if count & (count - 1) == 0:
        return index ^ step
    return (index + step) % count


def exchanged(parts, axis):
    count = lax.axis_size(axis)
    brought = []
    for step, part in enumerate(parts, 1):
        pairs = [(index, target(index, step, count)) for index in range(count)]
        brought.append(lax.ppermute(part, axis, pairs))
    return brought


def add_kernel(*refs):
    *parts, out_ref = refs
    total = [widen(part[...]) for part in parts]
    while len(total) > 1:
        total = [sum(total[n : n + 2][1:], total[n]) for n in range(0, len(total), 2)]
    out_ref[...] = total[0].astype(out_ref.dtype)


def added(parts, dtype):
    return pl.pallas_call(
        add_kernel,
        in_specs=[VMEM] * len(parts),
        out_specs=VMEM,
        out_shape=jax.ShapeDtypeStruct(parts[0].shape, dtype),
        name="add",
        compiler_params=pltpu.CompilerParams(vmem_limit_bytes=LIMIT * 1024 * 1024),
    )(*parts)


def brought(value, step):
    axes = ("ctx", "dp")
    count = lax.axis_size("ctx") * lax.axis_size("dp")
    return lax.ppermute(value, axes, [(index, index ^ step) for index in range(count)])


def windows(rows, blocks, height):
    return jnp.concatenate([rows[BLOCK * b : BLOCK * b + height] for b in range(blocks)], axis=1)


def bands(base, count, width):
    rows = []
    for group in range(count):
        row = jnp.broadcast_to(base[group : group + 1, :], (BLOCK, base.shape[1]))
        row = pltpu.roll(row, 0, 1, stride=1, stride_axis=0)
        rows.append(row[:, :width].astype(jnp.bfloat16))
    return jnp.concatenate(rows, axis=0)


def convolved(base, window, blocks, taps, group_width):
    count = LANES // group_width
    every = jnp.dot(
        bands(base, count, taps + BLOCK),
        windows(window, blocks, taps + BLOCK),
        preferred_element_type=jnp.float32,
    )
    lane_group = lax.broadcasted_iota(jnp.int32, (BLOCK, LANES), 1) // group_width
    outs = []
    for b in range(blocks):
        columns = slice(b * LANES, (b + 1) * LANES)
        out = every[:BLOCK, columns]
        for group in range(1, count):
            out = jnp.where(
                lane_group == group, every[group * BLOCK : (group + 1) * BLOCK, columns], out
            )
        outs.append(out)
    return jnp.concatenate(outs, axis=0)


def tiles(channels, group_width):
    count = LANES // group_width
    for tile in range(channels // LANES):
        yield slice(tile * LANES, (tile + 1) * LANES), slice(tile * count, (tile + 1) * count)


def send_out(stage_ref, out_ref, sem, c):
    if c.stop % STEP == 0 or c.stop == stage_ref.shape[1]:
        begin = (c.stop - 1) // STEP * STEP
        columns = pl.ds(begin, c.stop - begin)
        copy = pltpu.make_async_copy(
            stage_ref.at[:, columns], out_ref.at[:, columns], sem.at[begin // STEP]
        )
        copy.start()
        return [copy]
    return []


def pack_kernel(count, grad_ref, k_ref, v_ref, *refs):
    parts, (tail_ref, k_stage, v_stage, part_sem, tail_sem) = refs[:count], refs[count:]
    here = lax.axis_index("tp")
    height = k_stage.shape[0]
    width = parts[0].shape[1]
    below = pl.ds(k_ref.shape[0] - height, height)
    tails = [
        pltpu.make_async_copy(ref.at[below], into, tail_sem.at[n])
        for n, (ref, into) in enumerate([(k_ref, k_stage), (v_ref, v_stage)])
    ]
    cuts = []
    for n, part in enumerate(parts):
        place = target(here, n, count) * width
        columns = pl.ds(pl.multiple_of(place, width), width)
        cuts.append(pltpu.make_async_copy(grad_ref.at[:, columns], part, part_sem.at[n]))
    for copy in tails + cuts:
        copy.start()
    for copy in tails:
        copy.wait()
    tail_ref[...] = product(k_stage[...], v_stage[...])
    for copy in cuts:
        copy.wait()


def gather_kernel(count, q_ref, *refs):
    parts, og_refs, head_ref = refs[:count], refs[count:-1], refs[-1]
    height, width = parts[0].shape
    piece = width // HALVES
    here = lax.axis_index("tp")
    head = head_ref.shape[0]
    for half, og_ref in enumerate(og_refs):
        c = slice(half * piece, (half + 1) * piece)
        for step, part in enumerate(parts):
            place = partner(here, step, count)
            og_ref[pl.ds(pl.multiple_of(place * height, height), height), :] = part[:, c]
        head_ref[:, c] = product(og_ref[:head, :], q_ref[:head, c])


def columns_of(refs, c):
    width = refs[0].shape[1]
    half = c.start // width
    return refs[half][:, c.start - half * width : c.stop - half * width]


def scores_kernel(taps, group_width, inner, q_ref, *refs):
    og_refs, (k_ref, v_ref, *more_refs, out_ref) = refs[:HALVES], refs[HALVES:]
    first, last = (taps, k_ref.shape[0]) if inner else (0, taps)
    blocks = (last - first) // BLOCK
    count = LANES // group_width
    upward = 7 - lax.broadcasted_iota(jnp.int32, (8, LANES), 0)
    lane = lax.broadcasted_iota(jnp.int32, (BLOCK, blocks * LANES), 1)
    lane_group = (lane % LANES) // group_width
    for c, rows in tiles(k_ref.shape[1], group_width):
        grad_mix = widen(columns_of(og_refs, c)[first:last]) * widen(q_ref[first:last, c])
        turned = []
        for b in range(blocks):
            for end in range((b + 1) * BLOCK, b * BLOCK, -8):
                eight = grad_mix[end - 8 : end]
                turned.append(jnp.take_along_axis(eight, upward, axis=0, mode="promise_in_bounds"))
        own = windows(jnp.concatenate(turned, axis=0).astype(jnp.bfloat16), blocks, BLOCK)
        window = product(k_ref[:last, c], v_ref[:last, c])
        if not inner:
            window = jnp.concatenate([more_refs[0][:, c], window], axis=0)
        split = [jnp.where(lane_group == g, own, jnp.zeros_like(own)) for g in range(count)]
        scores = lax.dot_general(
            jnp.concatenate(split, axis=0),
            windows(window, blocks, taps + BLOCK),
            (((1,), (1,)), ((), ())),
            preferred_element_type=jnp.float32,
        )
        spare = jnp.zeros((scores.shape[0], 2 * taps - scores.shape[1]), jnp.float32)
        scores = jnp.concatenate([scores, spare], axis=1)
        sums = []
        for g in range(count):
            lags = scores[g * BLOCK : (g + 1) * BLOCK]
            lags = pltpu.roll(lags, taps - BLOCK, 1, stride=1, stride_axis=0)[:, taps:]
            sums.append(jnp.sum(lags, axis=0, keepdims=True))
        sums = jnp.concatenate(sums, axis=0)
        out_ref[rows, :] = sums if inner else (sums + more_refs[1][rows, :]).astype(out_ref.dtype)


def turned_base(filter_ref):
    taps = filter_ref.shape[1]
    tap = lax.broadcasted_iota(jnp.int32, (taps, 2 * taps), 0)
    place = lax.broadcasted_iota(jnp.int32, (taps, 2 * taps), 1)
    turn = (tap + place == taps).astype(jnp.bfloat16)
    return jnp.dot(filter_ref[...].astype(jnp.bfloat16), turn, preferred_element_type=jnp.float32)


def inner_mixed_kernel(taps, group_width, k_ref, v_ref, filter_ref, out_ref):
    blocks = (k_ref.shape[0] - taps) // BLOCK
    base = turned_base(filter_ref)
    for c, rows in tiles(k_ref.shape[1], group_width):
        window = product(k_ref[:, c], v_ref[:, c])
        out_ref[:, c] = convolved(base[rows], window, blocks, taps, group_width)


def mixed_kernel(taps, group_width, k_ref, v_ref, early_ref, filter_ref, inner_ref, *refs):
    og_refs, (out_ref, stage_ref, sem) = refs[:HALVES], refs[HALVES:]
    blocks = taps // BLOCK
    base = turned_base(filter_ref)
    copies = []
    for c, rows in tiles(k_ref.shape[1], group_width):
        window = product(k_ref[:taps, c], v_ref[:taps, c])
        window = jnp.concatenate([early_ref[:, c], window], axis=0)
        mixed = convolved(base[rows], window, blocks, taps, group_width)
        og = columns_of(og_refs, c)
        stage_ref[:taps, c] = (widen(og[:taps]) * mixed).astype(jnp.bfloat16)
        stage_ref[taps:, c] = (widen(og[taps:]) * inner_ref[:, c]).astype(jnp.bfloat16)
        copies += send_out(stage_ref, out_ref, sem, c)
    for copy in copies:
        copy.wait()


def back_kernel(taps, group_width, q_ref, k_ref, v_ref, filter_ref, *refs):
    og_refs, refs = refs[:HALVES], refs[HALVES:]
    late_ref, kg_ref, vg_ref, k_stage, v_stage, k_sem, v_sem = refs
    blocks = k_ref.shape[0] // BLOCK
    coeffs = widen(filter_ref[...].astype(jnp.bfloat16))
    base = jnp.concatenate([coeffs, jnp.zeros_like(coeffs)], axis=1)
    copies = []
    for c, rows in tiles(k_ref.shape[1], group_width):
        grad_mix = product(columns_of(og_refs, c), q_ref[:, c])
        window = jnp.concatenate([grad_mix, late_ref[:, c]], axis=0)
        back = convolved(base[rows], window, blocks, taps, group_width)
        k_stage[:, c] = (back * widen(v_ref[:, c])).astype(jnp.bfloat16)
        v_stage[:, c] = (back * widen(k_ref[:, c])).astype(jnp.bfloat16)
        copies += send_out(k_stage, kg_ref, k_sem, c) + send_out(v_stage, vg_ref, v_sem, c)
    for copy in copies:
        copy.wait()


def call(kernel, name, args, outs, staged, cost):
    steps = -(-outs[0].shape[-1] // STEP)
    stages = [pltpu.VMEM(o.shape, o.dtype) for o in outs] + [pltpu.SemaphoreType.DMA((steps,)) for _ in outs]
    return pl.pallas_call(
        kernel,
        in_specs=[SCALAR if a.dtype == jnp.int32 else VMEM for a in args],
        out_specs=[ANYWHERE if staged else VMEM for _ in outs],
        out_shape=outs,
        scratch_shapes=stages if staged else [],
        name=name,
        cost_estimate=pl.CostEstimate(flops=cost, bytes_accessed=1000, transcendentals=0),
        compiler_params=pltpu.CompilerParams(vmem_limit_bytes=LIMIT * 1024 * 1024),
    )(*args)


def local(queries, keys, values, out_grad, filters):
    q, k, v = queries[0], keys[0], values[0]
    rows, channels = q.shape
    groups, taps = filters.shape
    group_width = channels // groups
    wide = jax.ShapeDtypeStruct((rows, channels), jnp.bfloat16)
    edge = jax.ShapeDtypeStruct((taps, channels), jnp.bfloat16)
    small = jax.ShapeDtypeStruct((groups, taps), jnp.float32)
    thin = jax.ShapeDtypeStruct((groups, taps), TRAVEL)
    half = jax.ShapeDtypeStruct((rows, channels // HALVES), jnp.bfloat16)
    count = lax.axis_size("tp")
    height = rows // count
    piece = jax.ShapeDtypeStruct((height, channels), jnp.bfloat16)
    *parts, tail = pl.pallas_call(
        functools.partial(pack_kernel, count),
        in_specs=[ANYWHERE] * 3,
        out_specs=[ANYWHERE] * count + [VMEM],
        out_shape=[piece] * count + [edge],
        scratch_shapes=[pltpu.VMEM(edge.shape, edge.dtype)] * 2
        + [pltpu.SemaphoreType.DMA((count,)), pltpu.SemaphoreType.DMA((2,))],
        name="pack",
        compiler_params=pltpu.CompilerParams(vmem_limit_bytes=LIMIT * 1024 * 1024),
    )(*[in_hbm(a) for a in (out_grad[0], k, v)])
    early = passed_along(tail, "ctx", 1)
    inner_rows = jax.ShapeDtypeStruct((rows - taps, channels), jnp.float32)
    (inner,) = call(
        functools.partial(inner_mixed_kernel, taps, group_width), "inner_causal", (k, v, filters), [inner_rows], False, COST
    )
    parts = parts[:1] + exchanged(parts[1:], "tp")
    parts, inner = lax.optimization_barrier((parts, inner))
    if height % 16 == 0:
        *grads, head = call(
            functools.partial(gather_kernel, count), "gather", (q, *parts), [half] * HALVES + [edge], False, 1000
        )
    else:
        here = lax.axis_index("tp")
        grad = jnp.zeros(wide.shape, wide.dtype)
        for step, part in enumerate(parts):
            place = partner(here, step, count)
            grad = lax.dynamic_update_slice_in_dim(grad, part, place * height, 0)
        head = product(grad[:taps], q[:taps])
        grads = jnp.split(grad, HALVES, axis=1)
    late = passed_along(head, "ctx", -1)
    work = functools.partial
    (lags,) = call(
        work(scores_kernel, taps, group_width, True), "inner_scores", (q, *grads, k, v), [small], False, COST
    )
    (lags,) = call(
        work(scores_kernel, taps, group_width, False), "edge_scores", (q, *grads, k, v, early, lags), [thin], False, COST
    )
    (query_grad,) = call(
        work(mixed_kernel, taps, group_width), "causal", (k, v, early, filters, inner, *grads), [wide], True, COST
    )
    lags = [lags] + [brought(lags, step) for step in FIRST]
    lags, query_grad = lax.optimization_barrier((lags, query_grad))
    lags = added(lags, TRAVEL)
    key_grad, value_grad = call(
        work(back_kernel, taps, group_width), "adjoint", (q, k, v, filters, *grads, late), [wide, wide], True, COST
    )
    lags = [lags] + [brought(lags, step) for step in SECOND]
    lags, key_grad = lax.optimization_barrier((lags, key_grad))
    lags = [widen(part) for part in lags]
    lags = (lags[0] + lags[1]) + (lags[2] + lags[3])
    scale = 1.0 / math.sqrt(lax.axis_size("dp") * lax.axis_size("ctx") * rows * group_width)
    return (query_grad[None], key_grad[None], value_grad[None], jnp.flip(lags, 1) * scale)


COST = 100_000_000
HALVES = 1
TRAVEL = jnp.bfloat16
FIRST = (1,)
SECOND = (2, 4, 6)
LIMIT = 8


def solution(mesh):
    in_specs = (
        P("dp", "ctx", "tp"),
        P("dp", "ctx", "tp"),
        P("dp", "ctx", "tp"),
        P("dp", ("ctx", "tp"), None),
        P("tp", None),
    )
    out_specs = (P("dp", "ctx", "tp"), P("dp", "ctx", "tp"), P("dp", "ctx", "tp"), P("tp", None))
    return jax.shard_map(local, mesh=mesh, in_specs=in_specs, out_specs=out_specs, check_vma=False)
```

```python
import functools
import math

import jax
import jax.numpy as jnp
from jax import lax
from jax.experimental import pallas as pl
from jax.experimental.pallas import tpu as pltpu
from jax.sharding import PartitionSpec as P

LANES = 128
BLOCK = 32
STEP = 4 * LANES
VMEM = pl.BlockSpec(memory_space=pltpu.VMEM)
ANYWHERE = pl.BlockSpec(memory_space=pl.ANY)
SCALAR = pl.BlockSpec(memory_space=pltpu.SMEM)


def in_hbm(value):
    return pltpu.with_memory_space_constraint(value, pltpu.HBM)


def widen(value):
    return value.astype(jnp.float32)


def product(left, right):
    return (widen(left) * widen(right)).astype(jnp.bfloat16)


def passed_along(value, axis, steps):
    count = lax.axis_size(axis)
    first, last = (max(0, -steps), min(count, count - steps))
    return lax.ppermute(value, axis, [(source, source + steps) for source in range(first, last)])


def passed_round(value, axis, steps):
    count = lax.axis_size(axis)
    return lax.ppermute(value, axis, [(index, (index + steps) % count) for index in range(count)])


def partner(index, step, count):
    if count & (count - 1) == 0:
        return index ^ step
    return (index - step + count) % count


def target(index, step, count):
    if count & (count - 1) == 0:
        return index ^ step
    return (index + step) % count


def exchanged(part, axis, step):
    count = lax.axis_size(axis)
    pairs = [(index, target(index, step, count)) for index in range(count)]
    return lax.ppermute(part, axis, pairs)


def add_kernel(*refs):
    *parts, out_ref = refs
    total = [widen(part[...]) for part in parts]
    while len(total) > 1:
        total = [sum(total[n : n + 2][1:], total[n]) for n in range(0, len(total), 2)]
    out_ref[...] = total[0].astype(out_ref.dtype)


def added(parts, dtype):
    return pl.pallas_call(
        add_kernel,
        in_specs=[VMEM] * len(parts),
        out_specs=VMEM,
        out_shape=jax.ShapeDtypeStruct(parts[0].shape, dtype),
        name="add",
        compiler_params=pltpu.CompilerParams(vmem_limit_bytes=LIMIT * 1024 * 1024),
    )(*parts)


def brought(value, step):
    axes = ("ctx", "dp")
    count = lax.axis_size("ctx") * lax.axis_size("dp")
    return lax.ppermute(value, axes, [(index, index ^ step) for index in range(count)])


def windows(rows, blocks, height):
    return jnp.concatenate([rows[BLOCK * b : BLOCK * b + height] for b in range(blocks)], axis=1)


def bands(base, count, width):
    rows = []
    for group in range(count):
        row = jnp.broadcast_to(base[group : group + 1, :], (BLOCK, base.shape[1]))
        row = pltpu.roll(row, 0, 1, stride=1, stride_axis=0)
        rows.append(row[:, :width].astype(jnp.bfloat16))
    return jnp.concatenate(rows, axis=0)


def convolved(base, window, blocks, taps, group_width):
    count = LANES // group_width
    every = jnp.dot(
        bands(base, count, taps + BLOCK),
        windows(window, blocks, taps + BLOCK),
        preferred_element_type=jnp.float32,
    )
    lane_group = lax.broadcasted_iota(jnp.int32, (BLOCK, LANES), 1) // group_width
    outs = []
    for b in range(blocks):
        columns = slice(b * LANES, (b + 1) * LANES)
        out = every[:BLOCK, columns]
        for group in range(1, count):
            out = jnp.where(
                lane_group == group, every[group * BLOCK : (group + 1) * BLOCK, columns], out
            )
        outs.append(out)
    return jnp.concatenate(outs, axis=0)


def tiles(channels, group_width):
    count = LANES // group_width
    for tile in range(channels // LANES):
        yield slice(tile * LANES, (tile + 1) * LANES), slice(tile * count, (tile + 1) * count)


def send_out(stage_ref, out_ref, sem, c):
    if c.stop % STEP == 0 or c.stop == stage_ref.shape[1]:
        begin = (c.stop - 1) // STEP * STEP
        columns = pl.ds(begin, c.stop - begin)
        copy = pltpu.make_async_copy(
            stage_ref.at[:, columns], out_ref.at[:, columns], sem.at[begin // STEP]
        )
        copy.start()
        return [copy]
    return []


def pack_kernel(count, last, grad_ref, k_ref, v_ref, *refs):
    parts, (tail_ref, k_stage, v_stage, part_sem, tail_sem) = refs[:-5], refs[-5:]
    here = lax.axis_index("tp")
    height = k_stage.shape[0]
    width = parts[0].shape[1]
    below = pl.ds(k_ref.shape[0] - height, height)
    tails = [
        pltpu.make_async_copy(ref.at[below], into, tail_sem.at[n])
        for n, (ref, into) in enumerate([(k_ref, k_stage), (v_ref, v_stage)])
    ]
    cuts = []
    for n, part in enumerate(parts):
        half, step = (0, n) if n < NEAR else divmod(n - NEAR, count - NEAR)
        step += 0 if n < NEAR else NEAR
        columns = part.shape[1]
        place = pl.multiple_of(target(here, step, count) * width + half * columns, columns)
        columns = pl.ds(place, columns)
        cuts.append(pltpu.make_async_copy(grad_ref.at[:, columns], part, part_sem.at[n]))
    for copy in tails + cuts:
        copy.start()
    for copy in tails:
        copy.wait()
    place = lax.axis_index("ctx")

    @pl.when(place == last)
    def _():
        tail_ref[...] = jnp.zeros(tail_ref.shape, tail_ref.dtype)

    @pl.when(place != last)
    def _():
        tail_ref[...] = product(k_stage[...], v_stage[...])

    for copy in cuts:
        copy.wait()


def gather_kernel(count, half, q_ref, *refs):
    parts, (og_ref, head_ref) = refs[:-2], refs[-2:]
    height, width = parts[-1].shape
    here = lax.axis_index("tp")
    head = head_ref.shape[0]
    c = slice(half * width, (half + 1) * width)
    for step, part in enumerate(parts):
        place = partner(here, step, count)
        rows = pl.ds(pl.multiple_of(place * height, height), height)
        og_ref[rows, :] = part[:, c] if step < NEAR else part[...]
    head_ref[...] = product(og_ref[:head, :], q_ref[:head, c])


def columns_of(refs, c):
    width = refs[0].shape[1]
    half = c.start // width
    return refs[half][:, c.start - half * width : c.stop - half * width]


def lag_sums(taps, group_width, grad_mix, window):
    blocks = grad_mix.shape[0] // BLOCK
    count = LANES // group_width
    upward = 7 - lax.broadcasted_iota(jnp.int32, (8, LANES), 0)
    lane = lax.broadcasted_iota(jnp.int32, (BLOCK, blocks * LANES), 1)
    lane_group = (lane % LANES) // group_width
    turned = []
    for b in range(blocks):
        for end in range((b + 1) * BLOCK, b * BLOCK, -8):
            eight = grad_mix[end - 8 : end]
            turned.append(jnp.take_along_axis(eight, upward, axis=0, mode="promise_in_bounds"))
    own = windows(jnp.concatenate(turned, axis=0).astype(jnp.bfloat16), blocks, BLOCK)
    split = [jnp.where(lane_group == g, own, jnp.zeros_like(own)) for g in range(count)]
    scores = lax.dot_general(
        jnp.concatenate(split, axis=0),
        windows(window, blocks, taps + BLOCK),
        (((1,), (1,)), ((), ())),
        preferred_element_type=jnp.float32,
    )
    spare = jnp.zeros((scores.shape[0], 2 * taps - scores.shape[1]), jnp.float32)
    scores = jnp.concatenate([scores, spare], axis=1)
    sums = []
    for g in range(count):
        lags = scores[g * BLOCK : (g + 1) * BLOCK]
        lags = pltpu.roll(lags, taps - BLOCK, 1, stride=1, stride_axis=0)[:, taps:]
        sums.append(jnp.sum(lags, axis=0, keepdims=True))
    return jnp.concatenate(sums, axis=0)


def inner_scores_kernel(taps, group_width, half, q_ref, og_ref, k_ref, v_ref, out_ref):
    begin = half * og_ref.shape[1]
    for own, rows in tiles(og_ref.shape[1], group_width):
        c = slice(begin + own.start, begin + own.stop)
        grad_mix = widen(og_ref[taps:, own]) * widen(q_ref[taps:, c])
        out_ref[rows, :] = lag_sums(taps, group_width, grad_mix, product(k_ref[:, c], v_ref[:, c]))


def scores_kernel(taps, group_width, q_ref, *refs):
    og_refs, (k_ref, v_ref, early_ref) = refs[:HALVES], refs[HALVES : HALVES + 3]
    inner_refs, out_ref = refs[HALVES + 3 : -1], refs[-1]
    height = inner_refs[0].shape[0]
    for c, rows in tiles(k_ref.shape[1], group_width):
        grad_mix = widen(columns_of(og_refs, c)[:taps]) * widen(q_ref[:taps, c])
        window = product(k_ref[:taps, c], v_ref[:taps, c])
        window = jnp.concatenate([early_ref[:, c], window], axis=0)
        half, first = divmod(rows.start, height)
        inner = inner_refs[half][first : first + rows.stop - rows.start, :]
        out_ref[rows, :] = lag_sums(taps, group_width, grad_mix, window) + inner


def turned_base(filter_ref):
    taps = filter_ref.shape[1]
    tap = lax.broadcasted_iota(jnp.int32, (taps, 2 * taps), 0)
    place = lax.broadcasted_iota(jnp.int32, (taps, 2 * taps), 1)
    turn = (tap + place == taps).astype(jnp.bfloat16)
    return jnp.dot(filter_ref[...].astype(jnp.bfloat16), turn, preferred_element_type=jnp.float32)


def inner_mixed_kernel(taps, group_width, k_ref, v_ref, filter_ref, out_ref):
    blocks = (k_ref.shape[0] - taps) // BLOCK
    base = turned_base(filter_ref)
    for c, rows in tiles(k_ref.shape[1], group_width):
        window = product(k_ref[:, c], v_ref[:, c])
        out_ref[:, c] = convolved(base[rows], window, blocks, taps, group_width)


def mixed_kernel(taps, group_width, k_ref, v_ref, early_ref, filter_ref, inner_ref, *refs):
    og_refs, (out_ref, stage_ref, sem) = refs[:HALVES], refs[HALVES:]
    blocks = taps // BLOCK
    base = turned_base(filter_ref)
    copies = []
    for c, rows in tiles(k_ref.shape[1], group_width):
        window = product(k_ref[:taps, c], v_ref[:taps, c])
        window = jnp.concatenate([early_ref[:, c], window], axis=0)
        mixed = convolved(base[rows], window, blocks, taps, group_width)
        og = columns_of(og_refs, c)
        stage_ref[:taps, c] = (widen(og[:taps]) * mixed).astype(jnp.bfloat16)
        stage_ref[taps:, c] = (widen(og[taps:]) * inner_ref[:, c]).astype(jnp.bfloat16)
        copies += send_out(stage_ref, out_ref, sem, c)
    for copy in copies:
        copy.wait()


def back_kernel(taps, group_width, q_ref, k_ref, v_ref, filter_ref, *refs):
    og_refs, late_refs, refs = refs[:HALVES], refs[HALVES : 2 * HALVES], refs[2 * HALVES :]
    kg_ref, vg_ref, k_stage, v_stage, k_sem, v_sem = refs
    blocks = k_ref.shape[0] // BLOCK
    coeffs = widen(filter_ref[...].astype(jnp.bfloat16))
    base = jnp.concatenate([coeffs, jnp.zeros_like(coeffs)], axis=1)
    copies = []
    for c, rows in tiles(k_ref.shape[1], group_width):
        grad_mix = product(columns_of(og_refs, c), q_ref[:, c])
        window = jnp.concatenate([grad_mix, columns_of(late_refs, c)], axis=0)
        back = convolved(base[rows], window, blocks, taps, group_width)
        k_stage[:, c] = (back * widen(v_ref[:, c])).astype(jnp.bfloat16)
        v_stage[:, c] = (back * widen(k_ref[:, c])).astype(jnp.bfloat16)
        copies += send_out(k_stage, kg_ref, k_sem, c) + send_out(v_stage, vg_ref, v_sem, c)
    for copy in copies:
        copy.wait()


def call(kernel, name, args, outs, staged, cost):
    steps = -(-outs[0].shape[-1] // STEP)
    stages = [pltpu.VMEM(o.shape, o.dtype) for o in outs] + [pltpu.SemaphoreType.DMA((steps,)) for _ in outs]
    return pl.pallas_call(
        kernel,
        in_specs=[SCALAR if a.dtype == jnp.int32 else VMEM for a in args],
        out_specs=[ANYWHERE if staged else VMEM for _ in outs],
        out_shape=outs,
        scratch_shapes=stages if staged else [],
        name=name,
        cost_estimate=pl.CostEstimate(flops=cost, bytes_accessed=1000, transcendentals=0),
        compiler_params=pltpu.CompilerParams(vmem_limit_bytes=LIMIT * 1024 * 1024),
    )(*args)


def local(queries, keys, values, out_grad, filters):
    q, k, v = queries[0], keys[0], values[0]
    rows, channels = q.shape
    groups, taps = filters.shape
    group_width = channels // groups
    wide = jax.ShapeDtypeStruct((rows, channels), jnp.bfloat16)
    edge = jax.ShapeDtypeStruct((taps, channels), jnp.bfloat16)
    small = jax.ShapeDtypeStruct((groups, taps), jnp.float32)
    half_small = jax.ShapeDtypeStruct((groups // HALVES, taps), jnp.float32)
    thin = jax.ShapeDtypeStruct((groups, taps), TRAVEL)
    width = channels // HALVES
    count = lax.axis_size("tp")
    height = rows // count
    far = count - NEAR
    pieces = [jax.ShapeDtypeStruct((height, channels), jnp.bfloat16)] * NEAR
    pieces += [jax.ShapeDtypeStruct((height, width), jnp.bfloat16)] * (HALVES * far)
    half_wide = jax.ShapeDtypeStruct((rows, width), jnp.bfloat16)
    half_edge = jax.ShapeDtypeStruct((taps, width), jnp.bfloat16)
    *parts, tail = pl.pallas_call(
        functools.partial(pack_kernel, count, lax.axis_size("ctx") - 1),
        in_specs=[ANYWHERE] * 3,
        out_specs=[ANYWHERE] * len(pieces) + [VMEM],
        out_shape=pieces + [edge],
        scratch_shapes=[pltpu.VMEM(edge.shape, edge.dtype)] * 2
        + [pltpu.SemaphoreType.DMA((len(pieces),)), pltpu.SemaphoreType.DMA((2,))],
        name="pack",
        compiler_params=pltpu.CompilerParams(vmem_limit_bytes=LIMIT * 1024 * 1024),
    )(*[in_hbm(a) for a in (out_grad[0], k, v)])
    early = passed_round(tail, "ctx", 1)
    near = parts[:1] + [exchanged(part, "tp", step) for step, part in enumerate(parts[1:NEAR], 1)]
    inner_rows = jax.ShapeDtypeStruct((rows - taps, channels), jnp.float32)
    (inner,) = call(
        functools.partial(inner_mixed_kernel, taps, group_width), "inner_causal", (k, v, filters), [inner_rows], False, COST
    )
    grads, heads, inners = [], [], []
    for half in range(HALVES):
        mine = parts[NEAR + half * far : NEAR + (half + 1) * far]
        if half:
            mine, near[-1] = lax.optimization_barrier((mine, near[-1]))
        brought_in = [exchanged(part, "tp", step) for step, part in enumerate(mine, NEAR)]
        if half:
            brought_in, inners[0] = lax.optimization_barrier((brought_in, inners[0]))
        else:
            brought_in, inner = lax.optimization_barrier((brought_in, inner))
        if height % 16 == 0:
            grad, head = call(
                functools.partial(gather_kernel, count, half), "gather", (q, *near, *brought_in),
                [half_wide, half_edge], False, 1000,
            )
        else:
            here = lax.axis_index("tp")
            c = slice(half * width, (half + 1) * width)
            grad = jnp.zeros(half_wide.shape, half_wide.dtype)
            for step, part in enumerate([part[:, c] for part in near] + brought_in):
                place = partner(here, step, count)
                grad = lax.dynamic_update_slice_in_dim(grad, part, place * height, 0)
            head = product(grad[:taps], q[:taps, c])
        grads.append(grad)
        heads.append(head)
        (lags,) = call(
            functools.partial(inner_scores_kernel, taps, group_width, half), "inner_scores", (q, grad, k, v), [half_small], False, COST
        )
        inners.append(lags)
    work = functools.partial
    (lags,) = call(
        work(scores_kernel, taps, group_width), "edge_scores", (q, *grads, k, v, early, *inners), [small], False, COST
    )
    lates = [passed_along(head, "ctx", -1) for head in heads]
    (query_grad,) = call(
        work(mixed_kernel, taps, group_width), "causal", (k, v, early, filters, inner, *grads), [wide], True, COST
    )
    lags = [lags] + [brought(lags, step) for step in FIRST]
    lags, query_grad = lax.optimization_barrier((lags, query_grad))
    lags = added(lags, TRAVEL)
    key_grad, value_grad = call(
        work(back_kernel, taps, group_width), "adjoint", (q, k, v, filters, *grads, *lates), [wide, wide], True, COST
    )
    lags = [lags] + [brought(lags, step) for step in SECOND]
    lags, key_grad = lax.optimization_barrier((lags, key_grad))
    lags = [widen(part) for part in lags]
    lags = (lags[0] + lags[1]) + (lags[2] + lags[3])
    scale = 1.0 / math.sqrt(lax.axis_size("dp") * lax.axis_size("ctx") * rows * group_width)
    return (query_grad[None], key_grad[None], value_grad[None], jnp.flip(lags, 1) * scale)


COST = 100_000_000
HALVES = 2
NEAR = 2
TRAVEL = jnp.bfloat16
FIRST = (1,)
SECOND = (2, 4, 6)
LIMIT = 8


def solution(mesh):
    in_specs = (
        P("dp", "ctx", "tp"),
        P("dp", "ctx", "tp"),
        P("dp", "ctx", "tp"),
        P("dp", ("ctx", "tp"), None),
        P("tp", None),
    )
    out_specs = (P("dp", "ctx", "tp"), P("dp", "ctx", "tp"), P("dp", "ctx", "tp"), P("tp", None))
    return jax.shard_map(local, mesh=mesh, in_specs=in_specs, out_specs=out_specs, check_vma=False)
```

```python
import functools
import math

import jax
import jax.numpy as jnp
from jax import lax
from jax.experimental import pallas as pl
from jax.experimental.pallas import tpu as pltpu
from jax.sharding import PartitionSpec as P

LANES = 128
BLOCK = 32
STEP = 1 * LANES
VMEM = pl.BlockSpec(memory_space=pltpu.VMEM)
ANYWHERE = pl.BlockSpec(memory_space=pl.ANY)
SCALAR = pl.BlockSpec(memory_space=pltpu.SMEM)


def in_hbm(value):
    return pltpu.with_memory_space_constraint(value, pltpu.HBM)


def widen(value):
    return value.astype(jnp.float32)


def product(left, right):
    return (widen(left) * widen(right)).astype(jnp.bfloat16)


def passed_along(value, axis, steps):
    count = lax.axis_size(axis)
    first, last = (max(0, -steps), min(count, count - steps))
    return lax.ppermute(value, axis, [(source, source + steps) for source in range(first, last)])


def passed_round(value, axis, steps):
    count = lax.axis_size(axis)
    return lax.ppermute(value, axis, [(index, (index + steps) % count) for index in range(count)])


def partner(index, step, count):
    if count & (count - 1) == 0:
        return index ^ step
    return (index - step + count) % count


def target(index, step, count):
    if count & (count - 1) == 0:
        return index ^ step
    return (index + step) % count


def exchanged(part, axis, step):
    count = lax.axis_size(axis)
    pairs = [(index, target(index, step, count)) for index in range(count)]
    return lax.ppermute(part, axis, pairs)


def add_kernel(*refs):
    *parts, out_ref = refs
    total = [widen(part[...]) for part in parts]
    while len(total) > 1:
        total = [sum(total[n : n + 2][1:], total[n]) for n in range(0, len(total), 2)]
    out_ref[...] = total[0].astype(out_ref.dtype)


def added(parts, dtype):
    return pl.pallas_call(
        add_kernel,
        in_specs=[VMEM] * len(parts),
        out_specs=VMEM,
        out_shape=jax.ShapeDtypeStruct(parts[0].shape, dtype),
        name="add",
        compiler_params=pltpu.CompilerParams(vmem_limit_bytes=LIMIT * 1024 * 1024),
    )(*parts)


def brought(value, step):
    axes = ("ctx", "dp")
    count = lax.axis_size("ctx") * lax.axis_size("dp")
    return lax.ppermute(value, axes, [(index, index ^ step) for index in range(count)])


def windows(rows, blocks, height):
    return jnp.concatenate([rows[BLOCK * b : BLOCK * b + height] for b in range(blocks)], axis=1)


def bands(base, count, width):
    rows = []
    for group in range(count):
        row = jnp.broadcast_to(base[group : group + 1, :], (BLOCK, base.shape[1]))
        row = pltpu.roll(row, 0, 1, stride=1, stride_axis=0)
        rows.append(row[:, :width].astype(jnp.bfloat16))
    return jnp.concatenate(rows, axis=0)


def convolved(base, window, blocks, taps, group_width):
    count = LANES // group_width
    every = jnp.dot(
        bands(base, count, taps + BLOCK),
        windows(window, blocks, taps + BLOCK),
        preferred_element_type=jnp.float32,
    )
    lane_group = lax.broadcasted_iota(jnp.int32, (BLOCK, LANES), 1) // group_width
    outs = []
    for b in range(blocks):
        columns = slice(b * LANES, (b + 1) * LANES)
        out = every[:BLOCK, columns]
        for group in range(1, count):
            out = jnp.where(
                lane_group == group, every[group * BLOCK : (group + 1) * BLOCK, columns], out
            )
        outs.append(out)
    return jnp.concatenate(outs, axis=0)


def tiles(channels, group_width):
    count = LANES // group_width
    for tile in range(channels // LANES):
        yield slice(tile * LANES, (tile + 1) * LANES), slice(tile * count, (tile + 1) * count)


def send_out(stage_ref, out_ref, sem, c):
    if c.stop % STEP == 0 or c.stop == stage_ref.shape[1]:
        begin = (c.stop - 1) // STEP * STEP
        columns = pl.ds(begin, c.stop - begin)
        copy = pltpu.make_async_copy(
            stage_ref.at[:, columns], out_ref.at[:, columns], sem.at[begin // STEP]
        )
        copy.start()
        return [copy]
    return []


def cut_out(cuts_of, count, grad_ref, parts, sem):
    here = lax.axis_index("tp")
    width = grad_ref.shape[1] // count
    cuts = []
    for n, ((step, half), part) in enumerate(zip(cuts_of, parts)):
        columns = part.shape[1]
        place = pl.multiple_of(target(here, step, count) * width + max(half, 0) * columns, columns)
        cuts.append(pltpu.make_async_copy(grad_ref.at[:, pl.ds(place, columns)], part, sem.at[n]))
    return cuts


def second_pack_kernel(cuts_of, count, grad_ref, *refs):
    cuts = cut_out(cuts_of, count, grad_ref, refs[:-1], refs[-1])
    for copy in cuts:
        copy.start()
    for copy in cuts:
        copy.wait()


def pack_kernel(cuts_of, count, last, grad_ref, k_ref, v_ref, *refs):
    parts, (tail_ref, k_stage, v_stage, part_sem, tail_sem) = refs[:-5], refs[-5:]
    height = k_stage.shape[0]
    below = pl.ds(k_ref.shape[0] - height, height)
    tails = [
        pltpu.make_async_copy(ref.at[below], into, tail_sem.at[n])
        for n, (ref, into) in enumerate([(k_ref, k_stage), (v_ref, v_stage)])
    ]
    cuts = cut_out(cuts_of, count, grad_ref, parts, part_sem)
    for copy in tails + cuts:
        copy.start()
    for copy in tails:
        copy.wait()
    place = lax.axis_index("ctx")

    @pl.when(place == last)
    def _():
        tail_ref[...] = jnp.zeros(tail_ref.shape, tail_ref.dtype)

    @pl.when(place != last)
    def _():
        tail_ref[...] = product(k_stage[...], v_stage[...])

    for copy in cuts:
        copy.wait()


def gather_kernel(count, half, q_ref, *refs):
    parts, (og_ref, head_ref) = refs[:-2], refs[-2:]
    height, width = parts[-1].shape
    here = lax.axis_index("tp")
    head = head_ref.shape[0]
    c = slice(half * width, (half + 1) * width)
    for step, part in enumerate(parts):
        place = partner(here, step, count)
        rows = pl.ds(pl.multiple_of(place * height, height), height)
        og_ref[rows, :] = part[:, c] if step < NEAR else part[...]
    head_ref[...] = product(og_ref[:head, :], q_ref[:head, c])


def columns_of(refs, c):
    width = refs[0].shape[1]
    half = c.start // width
    return refs[half][:, c.start - half * width : c.stop - half * width]


def lag_sums(taps, group_width, grad_mix, window):
    blocks = grad_mix.shape[0] // BLOCK
    count = LANES // group_width
    upward = 7 - lax.broadcasted_iota(jnp.int32, (8, LANES), 0)
    lane = lax.broadcasted_iota(jnp.int32, (BLOCK, blocks * LANES), 1)
    lane_group = (lane % LANES) // group_width
    turned = []
    for b in range(blocks):
        for end in range((b + 1) * BLOCK, b * BLOCK, -8):
            eight = grad_mix[end - 8 : end]
            turned.append(jnp.take_along_axis(eight, upward, axis=0, mode="promise_in_bounds"))
    own = windows(jnp.concatenate(turned, axis=0).astype(jnp.bfloat16), blocks, BLOCK)
    split = [jnp.where(lane_group == g, own, jnp.zeros_like(own)) for g in range(count)]
    scores = lax.dot_general(
        jnp.concatenate(split, axis=0),
        windows(window, blocks, taps + BLOCK),
        (((1,), (1,)), ((), ())),
        preferred_element_type=jnp.float32,
    )
    spare = jnp.zeros((scores.shape[0], 2 * taps - scores.shape[1]), jnp.float32)
    scores = jnp.concatenate([scores, spare], axis=1)
    sums = []
    for g in range(count):
        lags = scores[g * BLOCK : (g + 1) * BLOCK]
        lags = pltpu.roll(lags, taps - BLOCK, 1, stride=1, stride_axis=0)[:, taps:]
        sums.append(jnp.sum(lags, axis=0, keepdims=True))
    return jnp.concatenate(sums, axis=0)


def inner_scores_kernel(taps, group_width, half, q_ref, og_ref, k_ref, v_ref, out_ref):
    begin = half * og_ref.shape[1]
    for own, rows in tiles(og_ref.shape[1], group_width):
        c = slice(begin + own.start, begin + own.stop)
        grad_mix = widen(og_ref[taps:, own]) * widen(q_ref[taps:, c])
        out_ref[rows, :] = lag_sums(taps, group_width, grad_mix, product(k_ref[:, c], v_ref[:, c]))


def scores_kernel(taps, group_width, q_ref, *refs):
    og_refs, (k_ref, v_ref, early_ref, inner_ref, out_ref) = refs[:HALVES], refs[HALVES:]
    for c, rows in tiles(k_ref.shape[1], group_width):
        there = c.stop <= og_refs[0].shape[1]
        last = taps if there else k_ref.shape[0]
        grad_mix = widen(columns_of(og_refs, c)[:last]) * widen(q_ref[:last, c])
        window = product(k_ref[:last, c], v_ref[:last, c])
        window = jnp.concatenate([early_ref[:, c], window], axis=0)
        sums = lag_sums(taps, group_width, grad_mix, window)
        out_ref[rows, :] = sums + inner_ref[rows, :] if there else sums


def turned_base(filter_ref):
    taps = filter_ref.shape[1]
    tap = lax.broadcasted_iota(jnp.int32, (taps, 2 * taps), 0)
    place = lax.broadcasted_iota(jnp.int32, (taps, 2 * taps), 1)
    turn = (tap + place == taps).astype(jnp.bfloat16)
    return jnp.dot(filter_ref[...].astype(jnp.bfloat16), turn, preferred_element_type=jnp.float32)


def inner_mixed_kernel(taps, group_width, k_ref, v_ref, filter_ref, out_ref):
    blocks = (k_ref.shape[0] - taps) // BLOCK
    base = turned_base(filter_ref)
    for c, rows in tiles(k_ref.shape[1], group_width):
        window = product(k_ref[:, c], v_ref[:, c])
        out_ref[:, c] = convolved(base[rows], window, blocks, taps, group_width)


def mixed_kernel(taps, group_width, k_ref, v_ref, early_ref, filter_ref, inner_ref, *refs):
    og_refs, (out_ref, stage_ref, sem) = refs[:HALVES], refs[HALVES:]
    blocks = taps // BLOCK
    base = turned_base(filter_ref)
    copies = []
    for c, rows in tiles(k_ref.shape[1], group_width):
        window = product(k_ref[:taps, c], v_ref[:taps, c])
        window = jnp.concatenate([early_ref[:, c], window], axis=0)
        mixed = convolved(base[rows], window, blocks, taps, group_width)
        og = columns_of(og_refs, c)
        stage_ref[:taps, c] = (widen(og[:taps]) * mixed).astype(jnp.bfloat16)
        stage_ref[taps:, c] = (widen(og[taps:]) * inner_ref[:, c]).astype(jnp.bfloat16)
        copies += send_out(stage_ref, out_ref, sem, c)
    for copy in copies:
        copy.wait()


def back_kernel(taps, group_width, q_ref, k_ref, v_ref, filter_ref, *refs):
    og_refs, late_refs, refs = refs[:HALVES], refs[HALVES : 2 * HALVES], refs[2 * HALVES :]
    kg_ref, vg_ref, k_stage, v_stage, k_sem, v_sem = refs
    blocks = k_ref.shape[0] // BLOCK
    coeffs = widen(filter_ref[...].astype(jnp.bfloat16))
    base = jnp.concatenate([coeffs, jnp.zeros_like(coeffs)], axis=1)
    copies = []
    for c, rows in tiles(k_ref.shape[1], group_width):
        grad_mix = product(columns_of(og_refs, c), q_ref[:, c])
        window = jnp.concatenate([grad_mix, columns_of(late_refs, c)], axis=0)
        back = convolved(base[rows], window, blocks, taps, group_width)
        k_stage[:, c] = (back * widen(v_ref[:, c])).astype(jnp.bfloat16)
        v_stage[:, c] = (back * widen(k_ref[:, c])).astype(jnp.bfloat16)
        copies += send_out(k_stage, kg_ref, k_sem, c) + send_out(v_stage, vg_ref, v_sem, c)
    for copy in copies:
        copy.wait()


def call(kernel, name, args, outs, staged, cost):
    steps = -(-outs[0].shape[-1] // STEP)
    stages = [pltpu.VMEM(o.shape, o.dtype) for o in outs] + [pltpu.SemaphoreType.DMA((steps,)) for _ in outs]
    return pl.pallas_call(
        kernel,
        in_specs=[SCALAR if a.dtype == jnp.int32 else VMEM for a in args],
        out_specs=[ANYWHERE if staged else VMEM for _ in outs],
        out_shape=outs,
        scratch_shapes=stages if staged else [],
        name=name,
        cost_estimate=pl.CostEstimate(flops=cost, bytes_accessed=1000, transcendentals=0),
        compiler_params=pltpu.CompilerParams(vmem_limit_bytes=LIMIT * 1024 * 1024),
    )(*args)


def local(queries, keys, values, out_grad, filters):
    q, k, v = queries[0], keys[0], values[0]
    rows, channels = q.shape
    groups, taps = filters.shape
    group_width = channels // groups
    wide = jax.ShapeDtypeStruct((rows, channels), jnp.bfloat16)
    edge = jax.ShapeDtypeStruct((taps, channels), jnp.bfloat16)
    small = jax.ShapeDtypeStruct((groups, taps), jnp.float32)
    half_small = jax.ShapeDtypeStruct((groups // HALVES, taps), jnp.float32)
    thin = jax.ShapeDtypeStruct((groups, taps), TRAVEL)
    width = channels // HALVES
    count = lax.axis_size("tp")
    height = rows // count
    far = count - NEAR
    piece = jax.ShapeDtypeStruct((height, channels), jnp.bfloat16)
    half_piece = jax.ShapeDtypeStruct((height, width), jnp.bfloat16)
    first_cuts = [(step, -1) for step in range(1, NEAR)] + [(step, 0) for step in range(NEAR, count)]
    second_cuts = [(0, -1)] + [(step, 1) for step in range(NEAR, count)]
    pieces = [half_piece if half >= 0 else piece for _, half in first_cuts]
    second_pieces = [half_piece if half >= 0 else piece for _, half in second_cuts]
    half_wide = jax.ShapeDtypeStruct((rows, width), jnp.bfloat16)
    half_edge = jax.ShapeDtypeStruct((taps, width), jnp.bfloat16)
    *parts, tail = pl.pallas_call(
        functools.partial(pack_kernel, first_cuts, count, lax.axis_size("ctx") - 1),
        in_specs=[ANYWHERE] * 3,
        out_specs=[ANYWHERE] * len(pieces) + [VMEM],
        out_shape=pieces + [edge],
        scratch_shapes=[pltpu.VMEM(edge.shape, edge.dtype)] * 2
        + [pltpu.SemaphoreType.DMA((len(pieces),)), pltpu.SemaphoreType.DMA((2,))],
        name="pack",
        compiler_params=pltpu.CompilerParams(vmem_limit_bytes=LIMIT * 1024 * 1024),
    )(*[in_hbm(a) for a in (out_grad[0], k, v)])
    early = passed_round(tail, "ctx", 1)
    near = [exchanged(part, "tp", step) for step, part in enumerate(parts[: NEAR - 1], 1)]
    grad_in, near[-1] = lax.optimization_barrier((out_grad[0], near[-1]))
    own, *second_parts = pl.pallas_call(
        functools.partial(second_pack_kernel, second_cuts, count),
        in_specs=[ANYWHERE],
        out_specs=[ANYWHERE] * len(second_pieces),
        out_shape=second_pieces,
        scratch_shapes=[pltpu.SemaphoreType.DMA((len(second_pieces),))],
        name="second_pack",
        compiler_params=pltpu.CompilerParams(vmem_limit_bytes=LIMIT * 1024 * 1024),
    )(in_hbm(grad_in))
    near = [own] + near
    inner_rows = jax.ShapeDtypeStruct((rows - taps, channels), jnp.float32)
    (inner,) = call(
        functools.partial(inner_mixed_kernel, taps, group_width), "inner_causal", (k, v, filters), [inner_rows], False, COST
    )
    grads, heads, inners = [], [], []
    for half in range(HALVES):
        mine = second_parts if half else parts[NEAR - 1 :]
        brought_in = [exchanged(part, "tp", step) for step, part in enumerate(mine, NEAR)]
        if half:
            brought_in, inners[0] = lax.optimization_barrier((brought_in, inners[0]))
        else:
            brought_in, inner = lax.optimization_barrier((brought_in, inner))
        if height % 16 == 0:
            grad, head = call(
                functools.partial(gather_kernel, count, half), "gather", (q, *near, *brought_in),
                [half_wide, half_edge], False, 1000,
            )
        else:
            here = lax.axis_index("tp")
            c = slice(half * width, (half + 1) * width)
            grad = jnp.zeros(half_wide.shape, half_wide.dtype)
            for step, part in enumerate([part[:, c] for part in near] + brought_in):
                place = partner(here, step, count)
                grad = lax.dynamic_update_slice_in_dim(grad, part, place * height, 0)
            head = product(grad[:taps], q[:taps, c])
        grads.append(grad)
        heads.append(head)
        if not half:
            (lags,) = call(
                functools.partial(inner_scores_kernel, taps, group_width, 0), "inner_scores", (q, grad, k, v), [half_small], False, COST
            )
            inners.append(lags)
    work = functools.partial
    (lags,) = call(
        work(scores_kernel, taps, group_width), "edge_scores", (q, *grads, k, v, early, *inners), [small], False, COST
    )
    lates = [passed_along(head, "ctx", -1) for head in heads]
    (query_grad,) = call(
        work(mixed_kernel, taps, group_width), "causal", (k, v, early, filters, inner, *grads), [wide], True, COST
    )
    lags = [lags] + [brought(lags, step) for step in FIRST]
    lags, query_grad = lax.optimization_barrier((lags, query_grad))
    lags = added(lags, TRAVEL)
    key_grad, value_grad = call(
        work(back_kernel, taps, group_width), "adjoint", (q, k, v, filters, *grads, *lates), [wide, wide], True, COST
    )
    lags = [lags] + [brought(lags, step) for step in SECOND]
    lags, key_grad = lax.optimization_barrier((lags, key_grad))
    lags = [widen(part) for part in lags]
    lags = (lags[0] + lags[1]) + (lags[2] + lags[3])
    scale = 1.0 / math.sqrt(lax.axis_size("dp") * lax.axis_size("ctx") * rows * group_width)
    return (query_grad[None], key_grad[None], value_grad[None], jnp.flip(lags, 1) * scale)


COST = 100_000_000
HALVES = 2
NEAR = 2
TRAVEL = jnp.bfloat16
FIRST = (1,)
SECOND = (2, 4, 6)
LIMIT = 8


def solution(mesh):
    in_specs = (
        P("dp", "ctx", "tp"),
        P("dp", "ctx", "tp"),
        P("dp", "ctx", "tp"),
        P("dp", ("ctx", "tp"), None),
        P("tp", None),
    )
    out_specs = (P("dp", "ctx", "tp"), P("dp", "ctx", "tp"), P("dp", "ctx", "tp"), P("tp", None))
    return jax.shard_map(local, mesh=mesh, in_specs=in_specs, out_specs=out_specs, check_vma=False)
```

```python
import functools
import math

import jax
import jax.numpy as jnp
from jax import lax
from jax.experimental import pallas as pl
from jax.experimental.pallas import tpu as pltpu
from jax.sharding import PartitionSpec as P

LANES = 128
BLOCK = 32
STEP = 1 * LANES
VMEM = pl.BlockSpec(memory_space=pltpu.VMEM)
ANYWHERE = pl.BlockSpec(memory_space=pl.ANY)


def in_hbm(value):
    return pltpu.with_memory_space_constraint(value, pltpu.HBM)


def widen(value):
    return value.astype(jnp.float32)


def product(left, right):
    return (widen(left) * widen(right)).astype(jnp.bfloat16)


def passed_along(value, axis, steps):
    count = lax.axis_size(axis)
    first, last = (max(0, -steps), min(count, count - steps))
    return lax.ppermute(value, axis, [(source, source + steps) for source in range(first, last)])


def passed_round(value, axis, steps):
    count = lax.axis_size(axis)
    return lax.ppermute(value, axis, [(index, (index + steps) % count) for index in range(count)])


def partner(index, step, count):
    if count & (count - 1) == 0:
        return index ^ step
    return (index - step + count) % count


def target(index, step, count):
    if count & (count - 1) == 0:
        return index ^ step
    return (index + step) % count


def exchanged(part, axis, step):
    count = lax.axis_size(axis)
    pairs = [(index, target(index, step, count)) for index in range(count)]
    return lax.ppermute(part, axis, pairs)


def add_kernel(*refs):
    *parts, out_ref = refs
    total = [widen(part[...]) for part in parts]
    while len(total) > 1:
        total = [sum(total[n : n + 2][1:], total[n]) for n in range(0, len(total), 2)]
    out_ref[...] = total[0].astype(out_ref.dtype)


def added(parts, dtype):
    return pl.pallas_call(
        add_kernel,
        in_specs=[VMEM] * len(parts),
        out_specs=VMEM,
        out_shape=jax.ShapeDtypeStruct(parts[0].shape, dtype),
        name="add",
        compiler_params=pltpu.CompilerParams(vmem_limit_bytes=LIMIT * 1024 * 1024),
    )(*parts)


def brought(value, step):
    axes = ("ctx", "dp")
    count = lax.axis_size("ctx") * lax.axis_size("dp")
    return lax.ppermute(value, axes, [(index, index ^ step) for index in range(count)])


def windows(rows, blocks, height):
    return jnp.concatenate([rows[BLOCK * b : BLOCK * b + height] for b in range(blocks)], axis=1)


def bands(base, count, width):
    rows = []
    for group in range(count):
        row = jnp.broadcast_to(base[group : group + 1, :], (BLOCK, base.shape[1]))
        row = pltpu.roll(row, 0, 1, stride=1, stride_axis=0)
        rows.append(row[:, :width].astype(jnp.bfloat16))
    return jnp.concatenate(rows, axis=0)


def convolved(base, window, blocks, taps, group_width):
    count = LANES // group_width
    every = jnp.dot(
        bands(base, count, taps + BLOCK),
        windows(window, blocks, taps + BLOCK),
        preferred_element_type=jnp.float32,
    )
    lane_group = lax.broadcasted_iota(jnp.int32, (BLOCK, LANES), 1) // group_width
    outs = []
    for b in range(blocks):
        columns = slice(b * LANES, (b + 1) * LANES)
        out = every[:BLOCK, columns]
        for group in range(1, count):
            out = jnp.where(
                lane_group == group, every[group * BLOCK : (group + 1) * BLOCK, columns], out
            )
        outs.append(out)
    return jnp.concatenate(outs, axis=0)


def tiles(channels, group_width):
    count = LANES // group_width
    for tile in range(channels // LANES):
        yield slice(tile * LANES, (tile + 1) * LANES), slice(tile * count, (tile + 1) * count)


def send_out(stage_ref, out_ref, sem, c, shift):
    if c.stop % STEP == 0 or c.stop == stage_ref.shape[1]:
        begin = (c.stop - 1) // STEP * STEP
        columns = pl.ds(begin, c.stop - begin)
        copy = pltpu.make_async_copy(
            stage_ref.at[:, columns],
            out_ref.at[:, pl.ds(shift + begin, c.stop - begin)],
            sem.at[begin // STEP],
        )
        copy.start()
        return [copy]
    return []


def cut_out(cuts_of, count, grad_ref, parts, sem):
    here = lax.axis_index("tp")
    width = grad_ref.shape[1] // count
    cuts = []
    for n, ((step, half), part) in enumerate(zip(cuts_of, parts)):
        columns = part.shape[1]
        place = pl.multiple_of(target(here, step, count) * width + max(half, 0) * columns, columns)
        cuts.append(pltpu.make_async_copy(grad_ref.at[:, pl.ds(place, columns)], part, sem.at[n]))
    return cuts


def second_pack_kernel(cuts_of, count, grad_ref, *refs):
    cuts = cut_out(cuts_of, count, grad_ref, refs[:-1], refs[-1])
    for copy in cuts:
        copy.start()
    for copy in cuts:
        copy.wait()


def pack_kernel(cuts_of, count, last, grad_ref, k_ref, v_ref, *refs):
    parts, (tail_ref, k_stage, v_stage, part_sem, tail_sem) = refs[:-5], refs[-5:]
    height = k_stage.shape[0]
    below = pl.ds(k_ref.shape[0] - height, height)
    tails = [
        pltpu.make_async_copy(ref.at[below], into, tail_sem.at[n])
        for n, (ref, into) in enumerate([(k_ref, k_stage), (v_ref, v_stage)])
    ]
    cuts = cut_out(cuts_of, count, grad_ref, parts, part_sem)
    for copy in tails + cuts:
        copy.start()
    for copy in tails:
        copy.wait()
    place = lax.axis_index("ctx")

    @pl.when(place == last)
    def _():
        tail_ref[...] = jnp.zeros(tail_ref.shape, tail_ref.dtype)

    @pl.when(place != last)
    def _():
        tail_ref[...] = product(k_stage[...], v_stage[...])

    for copy in cuts:
        copy.wait()


def gather_kernel(count, half, q_ref, *refs):
    parts, (og_ref, head_ref) = refs[:-2], refs[-2:]
    height, width = parts[-1].shape
    here = lax.axis_index("tp")
    head = head_ref.shape[0]
    c = slice(half * width, (half + 1) * width)
    for step, part in enumerate(parts):
        place = partner(here, step, count)
        rows = pl.ds(pl.multiple_of(place * height, height), height)
        og_ref[rows, :] = part[:, c] if step < NEAR else part[...]
    head_ref[...] = product(og_ref[:head, :], q_ref[:head, c])


def columns_of(refs, c):
    width = refs[0].shape[1]
    half = c.start // width
    return refs[half][:, c.start - half * width : c.stop - half * width]


def lag_sums(taps, group_width, grad_mix, window):
    blocks = grad_mix.shape[0] // BLOCK
    count = LANES // group_width
    upward = 7 - lax.broadcasted_iota(jnp.int32, (8, LANES), 0)
    lane = lax.broadcasted_iota(jnp.int32, (BLOCK, blocks * LANES), 1)
    lane_group = (lane % LANES) // group_width
    turned = []
    for b in range(blocks):
        for end in range((b + 1) * BLOCK, b * BLOCK, -8):
            eight = grad_mix[end - 8 : end]
            turned.append(jnp.take_along_axis(eight, upward, axis=0, mode="promise_in_bounds"))
    own = windows(jnp.concatenate(turned, axis=0).astype(jnp.bfloat16), blocks, BLOCK)
    split = [jnp.where(lane_group == g, own, jnp.zeros_like(own)) for g in range(count)]
    scores = lax.dot_general(
        jnp.concatenate(split, axis=0),
        windows(window, blocks, taps + BLOCK),
        (((1,), (1,)), ((), ())),
        preferred_element_type=jnp.float32,
    )
    spare = jnp.zeros((scores.shape[0], 2 * taps - scores.shape[1]), jnp.float32)
    scores = jnp.concatenate([scores, spare], axis=1)
    sums = []
    for g in range(count):
        lags = scores[g * BLOCK : (g + 1) * BLOCK]
        lags = pltpu.roll(lags, taps - BLOCK, 1, stride=1, stride_axis=0)[:, taps:]
        sums.append(jnp.sum(lags, axis=0, keepdims=True))
    return jnp.concatenate(sums, axis=0)


def inner_scores_kernel(taps, group_width, half, q_ref, og_ref, k_ref, v_ref, out_ref):
    begin = half * og_ref.shape[1]
    for own, rows in tiles(og_ref.shape[1], group_width):
        c = slice(begin + own.start, begin + own.stop)
        grad_mix = widen(og_ref[taps:, own]) * widen(q_ref[taps:, c])
        out_ref[rows, :] = lag_sums(taps, group_width, grad_mix, product(k_ref[:, c], v_ref[:, c]))


def scores_kernel(taps, group_width, q_ref, *refs):
    og_refs, (k_ref, v_ref, early_ref, inner_ref, out_ref) = refs[:HALVES], refs[HALVES:]
    for c, rows in tiles(k_ref.shape[1], group_width):
        there = c.stop <= og_refs[0].shape[1]
        last = taps if there else k_ref.shape[0]
        grad_mix = widen(columns_of(og_refs, c)[:last]) * widen(q_ref[:last, c])
        window = product(k_ref[:last, c], v_ref[:last, c])
        window = jnp.concatenate([early_ref[:, c], window], axis=0)
        sums = lag_sums(taps, group_width, grad_mix, window)
        sums = sums + inner_ref[rows, :] if there else sums
        out_ref[rows, :] = sums.astype(out_ref.dtype)


def turned_base(filter_ref):
    taps = filter_ref.shape[1]
    tap = lax.broadcasted_iota(jnp.int32, (taps, 2 * taps), 0)
    place = lax.broadcasted_iota(jnp.int32, (taps, 2 * taps), 1)
    turn = (tap + place == taps).astype(jnp.bfloat16)
    return jnp.dot(filter_ref[...].astype(jnp.bfloat16), turn, preferred_element_type=jnp.float32)


def inner_mixed_kernel(taps, group_width, k_ref, v_ref, filter_ref, out_ref):
    blocks = (k_ref.shape[0] - taps) // BLOCK
    base = turned_base(filter_ref)
    for c, rows in tiles(k_ref.shape[1], group_width):
        window = product(k_ref[:, c], v_ref[:, c])
        out_ref[:, c] = convolved(base[rows], window, blocks, taps, group_width)


def mixed_kernel(taps, group_width, k_ref, v_ref, early_ref, filter_ref, inner_ref, *refs):
    og_refs, out_ref = refs[:HALVES], refs[HALVES]
    blocks = taps // BLOCK
    base = turned_base(filter_ref)
    for c, rows in tiles(k_ref.shape[1], group_width):
        window = product(k_ref[:taps, c], v_ref[:taps, c])
        window = jnp.concatenate([early_ref[:, c], window], axis=0)
        mixed = convolved(base[rows], window, blocks, taps, group_width)
        og = columns_of(og_refs, c)
        out_ref[:taps, c] = (widen(og[:taps]) * mixed).astype(jnp.bfloat16)
        out_ref[taps:, c] = (widen(og[taps:]) * inner_ref[:, c]).astype(jnp.bfloat16)


def back_columns(taps, group_width, half, q_ref, k_ref, v_ref, filter_ref, og_ref, late_ref):
    blocks = k_ref.shape[0] // BLOCK
    coeffs = widen(filter_ref[...].astype(jnp.bfloat16))
    base = jnp.concatenate([coeffs, jnp.zeros_like(coeffs)], axis=1)
    begin = half * og_ref.shape[1]
    for own, _ in tiles(og_ref.shape[1], group_width):
        c = slice(begin + own.start, begin + own.stop)
        rows = slice(c.start // group_width, c.stop // group_width)
        window = jnp.concatenate([product(og_ref[:, own], q_ref[:, c]), late_ref[:, own]], axis=0)
        back = convolved(base[rows], window, blocks, taps, group_width)
        yield own, [(back * widen(ref[:, c])).astype(jnp.bfloat16) for ref in (v_ref, k_ref)]


def first_back_kernel(taps, group_width, *refs):
    inputs, (qg_ref, kg_ref, vg_ref, out_ref, sem) = refs[:6], refs[6:]
    copy = pltpu.make_async_copy(qg_ref, out_ref, sem)
    copy.start()
    for own, (kg, vg) in back_columns(taps, group_width, 0, *inputs):
        kg_ref[:, own] = kg
        vg_ref[:, own] = vg
    copy.wait()


def second_back_kernel(taps, group_width, *refs):
    inputs, refs = refs[:6], refs[6:]
    kg_first, vg_first, kg_ref, vg_ref, k_stage, v_stage, first_sem, k_sem, v_sem = refs
    width = kg_first.shape[1]
    first = pl.ds(0, width)
    copies = [
        pltpu.make_async_copy(kg_first, kg_ref.at[:, first], first_sem.at[0]),
        pltpu.make_async_copy(vg_first, vg_ref.at[:, first], first_sem.at[1]),
    ]
    for copy in copies:
        copy.start()
    for own, (kg, vg) in back_columns(taps, group_width, 1, *inputs):
        k_stage[:, own] = kg
        v_stage[:, own] = vg
        copies += send_out(k_stage, kg_ref, k_sem, own, width)
        copies += send_out(v_stage, vg_ref, v_sem, own, width)
    for copy in copies:
        copy.wait()


def call(kernel, name, args, outs, cost, in_hbm_from=None, scratch=()):
    kept = len(outs) if in_hbm_from is None else in_hbm_from
    return pl.pallas_call(
        kernel,
        in_specs=[VMEM] * len(args),
        out_specs=[VMEM] * kept + [ANYWHERE] * (len(outs) - kept),
        out_shape=outs,
        scratch_shapes=scratch,
        name=name,
        cost_estimate=pl.CostEstimate(flops=cost, bytes_accessed=1000, transcendentals=0),
        compiler_params=pltpu.CompilerParams(vmem_limit_bytes=LIMIT * 1024 * 1024),
    )(*args)


def local(queries, keys, values, out_grad, filters):
    q, k, v = queries[0], keys[0], values[0]
    rows, channels = q.shape
    groups, taps = filters.shape
    group_width = channels // groups
    wide = jax.ShapeDtypeStruct((rows, channels), jnp.bfloat16)
    edge = jax.ShapeDtypeStruct((taps, channels), jnp.bfloat16)
    small = jax.ShapeDtypeStruct((groups, taps), jnp.float32)
    half_small = jax.ShapeDtypeStruct((groups // HALVES, taps), jnp.float32)
    thin = jax.ShapeDtypeStruct((groups, taps), TRAVEL)
    width = channels // HALVES
    count = lax.axis_size("tp")
    height = rows // count
    far = count - NEAR
    piece = jax.ShapeDtypeStruct((height, channels), jnp.bfloat16)
    half_piece = jax.ShapeDtypeStruct((height, width), jnp.bfloat16)
    first_cuts = [(step, -1) for step in range(1, NEAR)] + [(step, 0) for step in range(NEAR, count)]
    second_cuts = [(0, -1)] + [(step, 1) for step in range(NEAR, count)]
    pieces = [half_piece if half >= 0 else piece for _, half in first_cuts]
    second_pieces = [half_piece if half >= 0 else piece for _, half in second_cuts]
    half_wide = jax.ShapeDtypeStruct((rows, width), jnp.bfloat16)
    half_edge = jax.ShapeDtypeStruct((taps, width), jnp.bfloat16)
    *parts, tail = pl.pallas_call(
        functools.partial(pack_kernel, first_cuts, count, lax.axis_size("ctx") - 1),
        in_specs=[ANYWHERE] * 3,
        out_specs=[ANYWHERE] * len(pieces) + [VMEM],
        out_shape=pieces + [edge],
        scratch_shapes=[pltpu.VMEM(edge.shape, edge.dtype)] * 2
        + [pltpu.SemaphoreType.DMA((len(pieces),)), pltpu.SemaphoreType.DMA((2,))],
        name="pack",
        compiler_params=pltpu.CompilerParams(vmem_limit_bytes=LIMIT * 1024 * 1024),
    )(*[in_hbm(a) for a in (out_grad[0], k, v)])
    early = passed_round(tail, "ctx", 1)
    near = [exchanged(part, "tp", step) for step, part in enumerate(parts[: NEAR - 1], 1)]
    grad_in, near[-1] = lax.optimization_barrier((out_grad[0], near[-1]))
    own, *second_parts = pl.pallas_call(
        functools.partial(second_pack_kernel, second_cuts, count),
        in_specs=[ANYWHERE],
        out_specs=[ANYWHERE] * len(second_pieces),
        out_shape=second_pieces,
        scratch_shapes=[pltpu.SemaphoreType.DMA((len(second_pieces),))],
        name="second_pack",
        compiler_params=pltpu.CompilerParams(vmem_limit_bytes=LIMIT * 1024 * 1024),
    )(in_hbm(grad_in))
    near = [own] + near
    inner_rows = jax.ShapeDtypeStruct((rows - taps, channels), jnp.float32)
    (inner,) = call(
        functools.partial(inner_mixed_kernel, taps, group_width), "inner_causal", (k, v, filters), [inner_rows], COST
    )
    grads, heads, inners = [], [], []
    for half in range(HALVES):
        mine = second_parts if half else parts[NEAR - 1 :]
        brought_in = [exchanged(part, "tp", step) for step, part in enumerate(mine, NEAR)]
        if half:
            brought_in, inners[0] = lax.optimization_barrier((brought_in, inners[0]))
        else:
            brought_in, inner = lax.optimization_barrier((brought_in, inner))
        if height % 16 == 0:
            grad, head = call(
                functools.partial(gather_kernel, count, half), "gather", (q, *near, *brought_in),
                [half_wide, half_edge], 1000,
            )
        else:
            here = lax.axis_index("tp")
            c = slice(half * width, (half + 1) * width)
            grad = jnp.zeros(half_wide.shape, half_wide.dtype)
            for step, part in enumerate([part[:, c] for part in near] + brought_in):
                place = partner(here, step, count)
                grad = lax.dynamic_update_slice_in_dim(grad, part, place * height, 0)
            head = product(grad[:taps], q[:taps, c])
        grads.append(grad)
        heads.append(head)
        if not half:
            (lags,) = call(
                functools.partial(inner_scores_kernel, taps, group_width, 0), "inner_scores", (q, grad, k, v), [half_small], COST
            )
            inners.append(lags)
    work = functools.partial
    (lags,) = call(
        work(scores_kernel, taps, group_width), "edge_scores", (q, *grads, k, v, early, *inners), [thin], COST
    )
    lates = [passed_along(head, "ctx", -1) for head in heads]
    (query_grad,) = call(
        work(mixed_kernel, taps, group_width), "causal", (k, v, early, filters, inner, *grads), [wide], COST
    )
    lags = [lags] + [brought(lags, step) for step in FIRST]
    lags, query_grad = lax.optimization_barrier((lags, query_grad))
    lags = added(lags, TRAVEL)
    sides = (q, k, v, filters)
    kept = jax.ShapeDtypeStruct((rows, width), jnp.bfloat16)
    key_first, value_first, query_grad = call(
        work(first_back_kernel, taps, group_width), "adjoint", (*sides, grads[0], lates[0], query_grad),
        [kept, kept, wide], COST_A, 2, [pltpu.SemaphoreType.DMA],
    )
    steps = pltpu.SemaphoreType.DMA((-(-width // STEP),))
    key_grad, value_grad = call(
        work(second_back_kernel, taps, group_width), "adjoint",
        (*sides, grads[1], lates[1], key_first, value_first), [wide, wide], COST_B, 0,
        [pltpu.VMEM(kept.shape, kept.dtype)] * 2 + [pltpu.SemaphoreType.DMA((2,)), steps, steps],
    )
    lags = [lags] + [brought(lags, step) for step in SECOND]
    lags, key_grad = lax.optimization_barrier((lags, key_grad))
    lags = [widen(part) for part in lags]
    lags = (lags[0] + lags[1]) + (lags[2] + lags[3])
    scale = 1.0 / math.sqrt(lax.axis_size("dp") * lax.axis_size("ctx") * rows * group_width)
    return (query_grad[None], key_grad[None], value_grad[None], jnp.flip(lags, 1) * scale)


COST = 100_000_000
COST_A = 100_000_000
COST_B = 1000
HALVES = 2
NEAR = 2
TRAVEL = jnp.bfloat16
FIRST = (1,)
SECOND = (2, 4, 6)
LIMIT = 8


def solution(mesh):
    in_specs = (
        P("dp", "ctx", "tp"),
        P("dp", "ctx", "tp"),
        P("dp", "ctx", "tp"),
        P("dp", ("ctx", "tp"), None),
        P("tp", None),
    )
    out_specs = (P("dp", "ctx", "tp"), P("dp", "ctx", "tp"), P("dp", "ctx", "tp"), P("tp", None))
    return jax.shard_map(local, mesh=mesh, in_specs=in_specs, out_specs=out_specs, check_vma=False)
```

```python
import functools
import math

import jax
import jax.numpy as jnp
from jax import lax
from jax.experimental import pallas as pl
from jax.experimental.pallas import tpu as pltpu
from jax.sharding import PartitionSpec as P

LANES = 128
BLOCK = 32
STEP = 1 * LANES
VMEM = pl.BlockSpec(memory_space=pltpu.VMEM)
ANYWHERE = pl.BlockSpec(memory_space=pl.ANY)


def in_hbm(value):
    return pltpu.with_memory_space_constraint(value, pltpu.HBM)


def widen(value):
    return value.astype(jnp.float32)


def product(left, right):
    return (widen(left) * widen(right)).astype(jnp.bfloat16)


def passed_along(value, axis, steps):
    count = lax.axis_size(axis)
    first, last = (max(0, -steps), min(count, count - steps))
    return lax.ppermute(value, axis, [(source, source + steps) for source in range(first, last)])


def passed_round(value, axis, steps):
    count = lax.axis_size(axis)
    return lax.ppermute(value, axis, [(index, (index + steps) % count) for index in range(count)])


def partner(index, step, count):
    if count & (count - 1) == 0:
        return index ^ step
    return (index - step + count) % count


def target(index, step, count):
    if count & (count - 1) == 0:
        return index ^ step
    return (index + step) % count


def exchanged(part, axis, step):
    count = lax.axis_size(axis)
    pairs = [(index, target(index, step, count)) for index in range(count)]
    return lax.ppermute(part, axis, pairs)


def add_kernel(*refs):
    *parts, out_ref = refs
    total = [widen(part[...]) for part in parts]
    while len(total) > 1:
        total = [sum(total[n : n + 2][1:], total[n]) for n in range(0, len(total), 2)]
    out_ref[...] = total[0].astype(out_ref.dtype)


def added(parts, dtype):
    return pl.pallas_call(
        add_kernel,
        in_specs=[VMEM] * len(parts),
        out_specs=VMEM,
        out_shape=jax.ShapeDtypeStruct(parts[0].shape, dtype),
        name="add",
        compiler_params=pltpu.CompilerParams(vmem_limit_bytes=LIMIT * 1024 * 1024),
    )(*parts)


def brought(value, step):
    axes = ("ctx", "dp")
    count = lax.axis_size("ctx") * lax.axis_size("dp")
    return lax.ppermute(value, axes, [(index, index ^ step) for index in range(count)])


def rounds_of_sum():
    rounds, base = [], 1
    for size in (lax.axis_size("dp"), lax.axis_size("ctx")):
        if size & (size - 1):
            return None
        while size > 1:
            width = 4 if size % 4 == 0 else 2
            rounds.append([base * step for step in range(1, width)])
            base *= width
            size //= width
    return rounds


def first_rounds(value, after):
    rounds = rounds_of_sum()
    if rounds is None:
        return lax.psum(widen(value), ("dp", "ctx")), after
    for n, steps in enumerate(rounds[:-1]):
        parts = [value] + [brought(value, step) for step in steps]
        if n == 0:
            parts, after = lax.optimization_barrier((parts, after))
        value = added(parts, TRAVEL if n == len(rounds) - 2 else jnp.float32)
    return value, after


def last_round(value, after):
    rounds = rounds_of_sum()
    if not rounds:
        return widen(value), after
    parts = [value] + [brought(value, step) for step in rounds[-1]]
    parts, after = lax.optimization_barrier((parts, after))
    parts = [widen(part) for part in parts]
    while len(parts) > 1:
        parts = [parts[m] + parts[m + 1] for m in range(0, len(parts), 2)]
    return parts[0], after


def windows(rows, blocks, height):
    return jnp.concatenate([rows[BLOCK * b : BLOCK * b + height] for b in range(blocks)], axis=1)


def bands(base, count, width):
    rows = []
    for group in range(count):
        row = jnp.broadcast_to(base[group : group + 1, :], (BLOCK, base.shape[1]))
        row = pltpu.roll(row, 0, 1, stride=1, stride_axis=0)
        rows.append(row[:, :width].astype(jnp.bfloat16))
    return jnp.concatenate(rows, axis=0)


def convolved(base, window, blocks, taps, group_width):
    count = LANES // group_width
    every = jnp.dot(
        bands(base, count, taps + BLOCK),
        windows(window, blocks, taps + BLOCK),
        preferred_element_type=jnp.float32,
    )
    lane_group = lax.broadcasted_iota(jnp.int32, (BLOCK, LANES), 1) // group_width
    outs = []
    for b in range(blocks):
        columns = slice(b * LANES, (b + 1) * LANES)
        out = every[:BLOCK, columns]
        for group in range(1, count):
            out = jnp.where(
                lane_group == group, every[group * BLOCK : (group + 1) * BLOCK, columns], out
            )
        outs.append(out)
    return jnp.concatenate(outs, axis=0)


def tiles(channels, group_width):
    count = LANES // group_width
    for tile in range(channels // LANES):
        yield slice(tile * LANES, (tile + 1) * LANES), slice(tile * count, (tile + 1) * count)


def send_out(stage_ref, out_ref, sem, c, shift):
    if c.stop % STEP == 0 or c.stop == stage_ref.shape[1]:
        begin = (c.stop - 1) // STEP * STEP
        columns = pl.ds(begin, c.stop - begin)
        copy = pltpu.make_async_copy(
            stage_ref.at[:, columns],
            out_ref.at[:, pl.ds(shift + begin, c.stop - begin)],
            sem.at[begin // STEP],
        )
        copy.start()
        return [copy]
    return []


def cut_out(cuts_of, count, grad_ref, parts, sem):
    here = lax.axis_index("tp")
    width = grad_ref.shape[1] // count
    cuts = []
    for n, ((step, half), part) in enumerate(zip(cuts_of, parts)):
        columns = part.shape[1]
        place = pl.multiple_of(target(here, step, count) * width + max(half, 0) * columns, columns)
        cuts.append(pltpu.make_async_copy(grad_ref.at[:, pl.ds(place, columns)], part, sem.at[n]))
    return cuts


def second_pack_kernel(cuts_of, count, grad_ref, *refs):
    cuts = cut_out(cuts_of, count, grad_ref, refs[:-1], refs[-1])
    for copy in cuts:
        copy.start()
    for copy in cuts:
        copy.wait()


def pack_kernel(cuts_of, count, last, grad_ref, k_ref, v_ref, *refs):
    parts, (tail_ref, k_stage, v_stage, part_sem, tail_sem) = refs[:-5], refs[-5:]
    height = k_stage.shape[0]
    below = pl.ds(k_ref.shape[0] - height, height)
    tails = [
        pltpu.make_async_copy(ref.at[below], into, tail_sem.at[n])
        for n, (ref, into) in enumerate([(k_ref, k_stage), (v_ref, v_stage)])
    ]
    cuts = cut_out(cuts_of, count, grad_ref, parts, part_sem)
    for copy in tails + cuts:
        copy.start()
    for copy in tails:
        copy.wait()
    place = lax.axis_index("ctx")

    @pl.when(place == last)
    def _():
        tail_ref[...] = jnp.zeros(tail_ref.shape, tail_ref.dtype)

    @pl.when(place != last)
    def _():
        tail_ref[...] = product(k_stage[...], v_stage[...])

    for copy in cuts:
        copy.wait()


def gather_kernel(count, half, q_ref, *refs):
    parts, (og_ref, head_ref) = refs[:-2], refs[-2:]
    height, width = parts[-1].shape
    here = lax.axis_index("tp")
    head = head_ref.shape[0]
    c = slice(half * width, (half + 1) * width)
    for step, part in enumerate(parts):
        place = partner(here, step, count)
        rows = pl.ds(pl.multiple_of(place * height, height), height)
        og_ref[rows, :] = part[:, c] if step < NEAR else part[...]
    head_ref[...] = product(og_ref[:head, :], q_ref[:head, c])


def columns_of(refs, c):
    width = refs[0].shape[1]
    half = c.start // width
    return refs[half][:, c.start - half * width : c.stop - half * width]


def lag_sums(taps, group_width, grad_mix, window):
    blocks = grad_mix.shape[0] // BLOCK
    count = LANES // group_width
    upward = 7 - lax.broadcasted_iota(jnp.int32, (8, LANES), 0)
    lane = lax.broadcasted_iota(jnp.int32, (BLOCK, blocks * LANES), 1)
    lane_group = (lane % LANES) // group_width
    turned = []
    for b in range(blocks):
        for end in range((b + 1) * BLOCK, b * BLOCK, -8):
            eight = grad_mix[end - 8 : end]
            turned.append(jnp.take_along_axis(eight, upward, axis=0, mode="promise_in_bounds"))
    own = windows(jnp.concatenate(turned, axis=0).astype(jnp.bfloat16), blocks, BLOCK)
    split = [jnp.where(lane_group == g, own, jnp.zeros_like(own)) for g in range(count)]
    scores = lax.dot_general(
        jnp.concatenate(split, axis=0),
        windows(window, blocks, taps + BLOCK),
        (((1,), (1,)), ((), ())),
        preferred_element_type=jnp.float32,
    )
    spare = jnp.zeros((scores.shape[0], 2 * taps - scores.shape[1]), jnp.float32)
    scores = jnp.concatenate([scores, spare], axis=1)
    sums = []
    for g in range(count):
        lags = scores[g * BLOCK : (g + 1) * BLOCK]
        lags = pltpu.roll(lags, taps - BLOCK, 1, stride=1, stride_axis=0)[:, taps:]
        sums.append(jnp.sum(lags, axis=0, keepdims=True))
    return jnp.concatenate(sums, axis=0)


def inner_scores_kernel(taps, group_width, half, q_ref, og_ref, k_ref, v_ref, out_ref):
    begin = half * og_ref.shape[1]
    for own, rows in tiles(og_ref.shape[1], group_width):
        c = slice(begin + own.start, begin + own.stop)
        grad_mix = widen(og_ref[taps:, own]) * widen(q_ref[taps:, c])
        out_ref[rows, :] = lag_sums(taps, group_width, grad_mix, product(k_ref[:, c], v_ref[:, c]))


def scores_kernel(taps, group_width, q_ref, *refs):
    og_refs, (k_ref, v_ref, early_ref, inner_ref, out_ref) = refs[:HALVES], refs[HALVES:]
    for c, rows in tiles(k_ref.shape[1], group_width):
        there = c.stop <= og_refs[0].shape[1]
        last = taps if there else k_ref.shape[0]
        grad_mix = widen(columns_of(og_refs, c)[:last]) * widen(q_ref[:last, c])
        window = product(k_ref[:last, c], v_ref[:last, c])
        window = jnp.concatenate([early_ref[:, c], window], axis=0)
        sums = lag_sums(taps, group_width, grad_mix, window)
        sums = sums + inner_ref[rows, :] if there else sums
        out_ref[rows, :] = sums.astype(out_ref.dtype)


def turned_base(filter_ref):
    taps = filter_ref.shape[1]
    tap = lax.broadcasted_iota(jnp.int32, (taps, 2 * taps), 0)
    place = lax.broadcasted_iota(jnp.int32, (taps, 2 * taps), 1)
    turn = (tap + place == taps).astype(jnp.bfloat16)
    return jnp.dot(filter_ref[...].astype(jnp.bfloat16), turn, preferred_element_type=jnp.float32)


def inner_mixed_kernel(taps, group_width, k_ref, v_ref, filter_ref, out_ref):
    blocks = (k_ref.shape[0] - taps) // BLOCK
    base = turned_base(filter_ref)
    for c, rows in tiles(k_ref.shape[1], group_width):
        window = product(k_ref[:, c], v_ref[:, c])
        out_ref[:, c] = convolved(base[rows], window, blocks, taps, group_width)


def mixed_kernel(taps, group_width, k_ref, v_ref, early_ref, filter_ref, inner_ref, *refs):
    og_refs, out_ref = refs[:HALVES], refs[HALVES]
    blocks = taps // BLOCK
    base = turned_base(filter_ref)
    for c, rows in tiles(k_ref.shape[1], group_width):
        window = product(k_ref[:taps, c], v_ref[:taps, c])
        window = jnp.concatenate([early_ref[:, c], window], axis=0)
        mixed = convolved(base[rows], window, blocks, taps, group_width)
        og = columns_of(og_refs, c)
        out_ref[:taps, c] = (widen(og[:taps]) * mixed).astype(jnp.bfloat16)
        out_ref[taps:, c] = (widen(og[taps:]) * inner_ref[:, c]).astype(jnp.bfloat16)


def back_columns(taps, group_width, half, q_ref, k_ref, v_ref, filter_ref, og_ref, late_ref):
    blocks = k_ref.shape[0] // BLOCK
    coeffs = widen(filter_ref[...].astype(jnp.bfloat16))
    base = jnp.concatenate([coeffs, jnp.zeros_like(coeffs)], axis=1)
    begin = half * og_ref.shape[1]
    for own, _ in tiles(og_ref.shape[1], group_width):
        c = slice(begin + own.start, begin + own.stop)
        rows = slice(c.start // group_width, c.stop // group_width)
        window = jnp.concatenate([product(og_ref[:, own], q_ref[:, c]), late_ref[:, own]], axis=0)
        back = convolved(base[rows], window, blocks, taps, group_width)
        yield own, [(back * widen(ref[:, c])).astype(jnp.bfloat16) for ref in (v_ref, k_ref)]


def first_back_kernel(taps, group_width, *refs):
    inputs, (qg_ref, kg_ref, vg_ref, out_ref, sem) = refs[:6], refs[6:]
    copy = pltpu.make_async_copy(qg_ref, out_ref, sem)
    copy.start()
    for own, (kg, vg) in back_columns(taps, group_width, 0, *inputs):
        kg_ref[:, own] = kg
        vg_ref[:, own] = vg
    copy.wait()


def second_back_kernel(taps, group_width, *refs):
    inputs, refs = refs[:6], refs[6:]
    kg_first, vg_first, kg_ref, vg_ref, k_stage, v_stage, first_sem, k_sem, v_sem = refs
    width = kg_first.shape[1]
    first = pl.ds(0, width)
    copies = [
        pltpu.make_async_copy(kg_first, kg_ref.at[:, first], first_sem.at[0]),
        pltpu.make_async_copy(vg_first, vg_ref.at[:, first], first_sem.at[1]),
    ]
    for copy in copies:
        copy.start()
    for own, (kg, vg) in back_columns(taps, group_width, 1, *inputs):
        k_stage[:, own] = kg
        v_stage[:, own] = vg
        copies += send_out(k_stage, kg_ref, k_sem, own, width)
        copies += send_out(v_stage, vg_ref, v_sem, own, width)
    for copy in copies:
        copy.wait()


def call(kernel, name, args, outs, cost, in_hbm_from=None, scratch=()):
    kept = len(outs) if in_hbm_from is None else in_hbm_from
    return pl.pallas_call(
        kernel,
        in_specs=[VMEM] * len(args),
        out_specs=[VMEM] * kept + [ANYWHERE] * (len(outs) - kept),
        out_shape=outs,
        scratch_shapes=scratch,
        name=name,
        cost_estimate=pl.CostEstimate(flops=cost, bytes_accessed=1000, transcendentals=0),
        compiler_params=pltpu.CompilerParams(vmem_limit_bytes=LIMIT * 1024 * 1024),
    )(*args)


def local(queries, keys, values, out_grad, filters):
    q, k, v = queries[0], keys[0], values[0]
    rows, channels = q.shape
    groups, taps = filters.shape
    group_width = channels // groups
    wide = jax.ShapeDtypeStruct((rows, channels), jnp.bfloat16)
    edge = jax.ShapeDtypeStruct((taps, channels), jnp.bfloat16)
    small = jax.ShapeDtypeStruct((groups, taps), jnp.float32)
    half_small = jax.ShapeDtypeStruct((groups // HALVES, taps), jnp.float32)
    thin = jax.ShapeDtypeStruct((groups, taps), TRAVEL)
    width = channels // HALVES
    count = lax.axis_size("tp")
    height = rows // count
    far = count - NEAR
    piece = jax.ShapeDtypeStruct((height, channels), jnp.bfloat16)
    half_piece = jax.ShapeDtypeStruct((height, width), jnp.bfloat16)
    first_cuts = [(step, -1) for step in range(1, NEAR)] + [(step, 0) for step in range(NEAR, count)]
    second_cuts = [(0, -1)] + [(step, 1) for step in range(NEAR, count)]
    pieces = [half_piece if half >= 0 else piece for _, half in first_cuts]
    second_pieces = [half_piece if half >= 0 else piece for _, half in second_cuts]
    half_wide = jax.ShapeDtypeStruct((rows, width), jnp.bfloat16)
    half_edge = jax.ShapeDtypeStruct((taps, width), jnp.bfloat16)
    *parts, tail = pl.pallas_call(
        functools.partial(pack_kernel, first_cuts, count, lax.axis_size("ctx") - 1),
        in_specs=[ANYWHERE] * 3,
        out_specs=[ANYWHERE] * len(pieces) + [VMEM],
        out_shape=pieces + [edge],
        scratch_shapes=[pltpu.VMEM(edge.shape, edge.dtype)] * 2
        + [pltpu.SemaphoreType.DMA((len(pieces),)), pltpu.SemaphoreType.DMA((2,))],
        name="pack",
        compiler_params=pltpu.CompilerParams(vmem_limit_bytes=LIMIT * 1024 * 1024),
    )(*[in_hbm(a) for a in (out_grad[0], k, v)])
    early = passed_round(tail, "ctx", 1)
    near = [exchanged(part, "tp", step) for step, part in enumerate(parts[: NEAR - 1], 1)]
    grad_in, near[-1] = lax.optimization_barrier((out_grad[0], near[-1]))
    own, *second_parts = pl.pallas_call(
        functools.partial(second_pack_kernel, second_cuts, count),
        in_specs=[ANYWHERE],
        out_specs=[ANYWHERE] * len(second_pieces),
        out_shape=second_pieces,
        scratch_shapes=[pltpu.SemaphoreType.DMA((len(second_pieces),))],
        name="second_pack",
        compiler_params=pltpu.CompilerParams(vmem_limit_bytes=LIMIT * 1024 * 1024),
    )(in_hbm(grad_in))
    near = [own] + near
    inner_rows = jax.ShapeDtypeStruct((rows - taps, channels), jnp.float32)
    (inner,) = call(
        functools.partial(inner_mixed_kernel, taps, group_width), "inner_causal", (k, v, filters), [inner_rows], COST
    )
    grads, heads, inners = [], [], []
    for half in range(HALVES):
        mine = second_parts if half else parts[NEAR - 1 :]
        brought_in = [exchanged(part, "tp", step) for step, part in enumerate(mine, NEAR)]
        if half:
            brought_in, inners[0] = lax.optimization_barrier((brought_in, inners[0]))
        else:
            brought_in, inner = lax.optimization_barrier((brought_in, inner))
        if height % 16 == 0:
            grad, head = call(
                functools.partial(gather_kernel, count, half), "gather", (q, *near, *brought_in),
                [half_wide, half_edge], 1000,
            )
        else:
            here = lax.axis_index("tp")
            c = slice(half * width, (half + 1) * width)
            grad = jnp.zeros(half_wide.shape, half_wide.dtype)
            for step, part in enumerate([part[:, c] for part in near] + brought_in):
                place = partner(here, step, count)
                grad = lax.dynamic_update_slice_in_dim(grad, part, place * height, 0)
            head = product(grad[:taps], q[:taps, c])
        grads.append(grad)
        heads.append(head)
        if not half:
            (lags,) = call(
                functools.partial(inner_scores_kernel, taps, group_width, 0), "inner_scores", (q, grad, k, v), [half_small], COST
            )
            inners.append(lags)
    work = functools.partial
    (lags,) = call(
        work(scores_kernel, taps, group_width), "edge_scores", (q, *grads, k, v, early, *inners), [small], COST
    )
    lates = [passed_along(head, "ctx", -1) for head in heads]
    (query_grad,) = call(
        work(mixed_kernel, taps, group_width), "causal", (k, v, early, filters, inner, *grads), [wide], COST
    )
    lags, query_grad = first_rounds(lags, query_grad)
    sides = (q, k, v, filters)
    kept = jax.ShapeDtypeStruct((rows, width), jnp.bfloat16)
    key_first, value_first, query_grad = call(
        work(first_back_kernel, taps, group_width), "adjoint", (*sides, grads[0], lates[0], query_grad),
        [kept, kept, wide], COST_A, 2, [pltpu.SemaphoreType.DMA],
    )
    steps = pltpu.SemaphoreType.DMA((-(-width // STEP),))
    key_grad, value_grad = call(
        work(second_back_kernel, taps, group_width), "adjoint",
        (*sides, grads[1], lates[1], key_first, value_first), [wide, wide], COST_B, 0,
        [pltpu.VMEM(kept.shape, kept.dtype)] * 2 + [pltpu.SemaphoreType.DMA((2,)), steps, steps],
    )
    lags, key_grad = last_round(lags, key_grad)
    scale = 1.0 / math.sqrt(lax.axis_size("dp") * lax.axis_size("ctx") * rows * group_width)
    return (query_grad[None], key_grad[None], value_grad[None], jnp.flip(lags, 1) * scale)


COST = 100_000_000
COST_A = 100_000_000
COST_B = 1000
HALVES = 2
NEAR = 2
TRAVEL = jnp.bfloat16
LIMIT = 8


def solution(mesh):
    in_specs = (
        P("dp", "ctx", "tp"),
        P("dp", "ctx", "tp"),
        P("dp", "ctx", "tp"),
        P("dp", ("ctx", "tp"), None),
        P("tp", None),
    )
    out_specs = (P("dp", "ctx", "tp"), P("dp", "ctx", "tp"), P("dp", "ctx", "tp"), P("tp", None))
    return jax.shard_map(local, mesh=mesh, in_specs=in_specs, out_specs=out_specs, check_vma=False)
```

```python
import functools
import math

import jax
import jax.numpy as jnp
from jax import lax
from jax.experimental import pallas as pl
from jax.experimental.pallas import tpu as pltpu
from jax.sharding import PartitionSpec as P

LANES = 128
BLOCK = 32
STEP = 1 * LANES
VMEM = pl.BlockSpec(memory_space=pltpu.VMEM)
ANYWHERE = pl.BlockSpec(memory_space=pl.ANY)


def in_hbm(value):
    return pltpu.with_memory_space_constraint(value, pltpu.HBM)


def widen(value):
    return value.astype(jnp.float32)


def product(left, right):
    return (widen(left) * widen(right)).astype(jnp.bfloat16)


def passed_along(value, axis, steps):
    count = lax.axis_size(axis)
    first, last = (max(0, -steps), min(count, count - steps))
    return lax.ppermute(value, axis, [(source, source + steps) for source in range(first, last)])


def passed_round(value, axis, steps):
    count = lax.axis_size(axis)
    return lax.ppermute(value, axis, [(index, (index + steps) % count) for index in range(count)])


def partner(index, step, count):
    if count & (count - 1) == 0:
        return index ^ step
    return (index - step + count) % count


def target(index, step, count):
    if count & (count - 1) == 0:
        return index ^ step
    return (index + step) % count


def exchanged(part, axis, step):
    count = lax.axis_size(axis)
    pairs = [(index, target(index, step, count)) for index in range(count)]
    return lax.ppermute(part, axis, pairs)


def add_kernel(*refs):
    *parts, out_ref = refs
    total = [widen(part[...]) for part in parts]
    while len(total) > 1:
        total = [sum(total[n : n + 2][1:], total[n]) for n in range(0, len(total), 2)]
    out_ref[...] = total[0].astype(out_ref.dtype)


def added(parts, dtype):
    return pl.pallas_call(
        add_kernel,
        in_specs=[VMEM] * len(parts),
        out_specs=VMEM,
        out_shape=jax.ShapeDtypeStruct(parts[0].shape, dtype),
        name="add",
        compiler_params=pltpu.CompilerParams(vmem_limit_bytes=LIMIT * 1024 * 1024),
    )(*parts)


def brought(value, step):
    axes = ("ctx", "dp")
    count = lax.axis_size("ctx") * lax.axis_size("dp")
    return lax.ppermute(value, axes, [(index, index ^ step) for index in range(count)])


def rounds_of_sum():
    rounds, base = [], 1
    for size in (lax.axis_size("dp"), lax.axis_size("ctx")):
        if size & (size - 1):
            return None
        while size > 1:
            width = 4 if size % 4 == 0 else 2
            rounds.append([base * step for step in range(1, width)])
            base *= width
            size //= width
    return rounds


def first_rounds(value, after):
    rounds = rounds_of_sum()
    if rounds is None:
        return lax.psum(widen(value), ("dp", "ctx")), after
    for n, steps in enumerate(rounds[:-1]):
        parts = [value] + [brought(value, step) for step in steps]
        if n == 0:
            parts, after = lax.optimization_barrier((parts, after))
        value = added(parts, TRAVEL if n == len(rounds) - 2 else jnp.float32)
    return value, after


def last_round(value, after):
    rounds = rounds_of_sum()
    if not rounds:
        return widen(value), after
    parts = [value] + [brought(value, step) for step in rounds[-1]]
    parts, after = lax.optimization_barrier((parts, after))
    parts = [widen(part) for part in parts]
    while len(parts) > 1:
        parts = [parts[m] + parts[m + 1] for m in range(0, len(parts), 2)]
    return parts[0], after


def windows(rows, blocks, height):
    return jnp.concatenate([rows[BLOCK * b : BLOCK * b + height] for b in range(blocks)], axis=1)


def bands(base, count, width):
    rows = []
    for group in range(count):
        row = jnp.broadcast_to(base[group : group + 1, :], (BLOCK, base.shape[1]))
        row = pltpu.roll(row, 0, 1, stride=1, stride_axis=0)
        rows.append(row[:, :width].astype(jnp.bfloat16))
    return jnp.concatenate(rows, axis=0)


def convolved(base, window, blocks, taps, group_width):
    count = LANES // group_width
    every = jnp.dot(
        bands(base, count, taps + BLOCK),
        windows(window, blocks, taps + BLOCK),
        preferred_element_type=jnp.float32,
    )
    lane_group = lax.broadcasted_iota(jnp.int32, (BLOCK, LANES), 1) // group_width
    outs = []
    for b in range(blocks):
        columns = slice(b * LANES, (b + 1) * LANES)
        out = every[:BLOCK, columns]
        for group in range(1, count):
            out = jnp.where(
                lane_group == group, every[group * BLOCK : (group + 1) * BLOCK, columns], out
            )
        outs.append(out)
    return jnp.concatenate(outs, axis=0)


def tiles(channels, group_width):
    count = LANES // group_width
    for tile in range(channels // LANES):
        yield slice(tile * LANES, (tile + 1) * LANES), slice(tile * count, (tile + 1) * count)


def send_out(stage_ref, out_ref, sem, c, below, right):
    if c.stop % STEP == 0 or c.stop == stage_ref.shape[1]:
        begin = (c.stop - 1) // STEP * STEP
        place = (pl.ds(below, stage_ref.shape[0]), pl.ds(right + begin, c.stop - begin))
        copy = pltpu.make_async_copy(
            stage_ref.at[:, pl.ds(begin, c.stop - begin)], out_ref.at[place], sem.at[begin // STEP]
        )
        copy.start()
        return [copy]
    return []


def cut_out(cuts_of, count, grad_ref, parts, sem):
    here = lax.axis_index("tp")
    width = grad_ref.shape[1] // count
    cuts = []
    for n, ((step, half), part) in enumerate(zip(cuts_of, parts)):
        columns = part.shape[1]
        place = pl.multiple_of(target(here, step, count) * width + max(half, 0) * columns, columns)
        cuts.append(pltpu.make_async_copy(grad_ref.at[:, pl.ds(place, columns)], part, sem.at[n]))
    return cuts


def second_pack_kernel(cuts_of, count, grad_ref, *refs):
    cuts = cut_out(cuts_of, count, grad_ref, refs[:-1], refs[-1])
    for copy in cuts:
        copy.start()
    for copy in cuts:
        copy.wait()


def pack_kernel(cuts_of, count, last, grad_ref, k_ref, v_ref, *refs):
    parts, (tail_ref, k_stage, v_stage, part_sem, tail_sem) = refs[:-5], refs[-5:]
    height = k_stage.shape[0]
    below = pl.ds(k_ref.shape[0] - height, height)
    tails = [
        pltpu.make_async_copy(ref.at[below], into, tail_sem.at[n])
        for n, (ref, into) in enumerate([(k_ref, k_stage), (v_ref, v_stage)])
    ]
    cuts = cut_out(cuts_of, count, grad_ref, parts, part_sem)
    for copy in tails + cuts:
        copy.start()
    for copy in tails:
        copy.wait()
    place = lax.axis_index("ctx")

    @pl.when(place == last)
    def _():
        tail_ref[...] = jnp.zeros(tail_ref.shape, tail_ref.dtype)

    @pl.when(place != last)
    def _():
        tail_ref[...] = product(k_stage[...], v_stage[...])

    for copy in cuts:
        copy.wait()


def gather_kernel(count, half, q_ref, *refs):
    parts, (og_ref, head_ref) = refs[:-2], refs[-2:]
    height, width = parts[-1].shape
    here = lax.axis_index("tp")
    head = head_ref.shape[0]
    c = slice(half * width, (half + 1) * width)
    for step, part in enumerate(parts):
        place = partner(here, step, count)
        rows = pl.ds(pl.multiple_of(place * height, height), height)
        og_ref[rows, :] = part[:, c] if step < NEAR else part[...]
    head_ref[...] = product(og_ref[:head, :], q_ref[:head, c])


def columns_of(refs, c):
    width = refs[0].shape[1]
    half = c.start // width
    return refs[half][:, c.start - half * width : c.stop - half * width]


def lag_sums(taps, group_width, grad_mix, window):
    blocks = grad_mix.shape[0] // BLOCK
    count = LANES // group_width
    upward = 7 - lax.broadcasted_iota(jnp.int32, (8, LANES), 0)
    lane = lax.broadcasted_iota(jnp.int32, (BLOCK, blocks * LANES), 1)
    lane_group = (lane % LANES) // group_width
    turned = []
    for b in range(blocks):
        for end in range((b + 1) * BLOCK, b * BLOCK, -8):
            eight = grad_mix[end - 8 : end]
            turned.append(jnp.take_along_axis(eight, upward, axis=0, mode="promise_in_bounds"))
    own = windows(jnp.concatenate(turned, axis=0).astype(jnp.bfloat16), blocks, BLOCK)
    split = [jnp.where(lane_group == g, own, jnp.zeros_like(own)) for g in range(count)]
    scores = lax.dot_general(
        jnp.concatenate(split, axis=0),
        windows(window, blocks, taps + BLOCK),
        (((1,), (1,)), ((), ())),
        preferred_element_type=jnp.float32,
    )
    spare = jnp.zeros((scores.shape[0], 2 * taps - scores.shape[1]), jnp.float32)
    scores = jnp.concatenate([scores, spare], axis=1)
    sums = []
    for g in range(count):
        lags = scores[g * BLOCK : (g + 1) * BLOCK]
        lags = pltpu.roll(lags, taps - BLOCK, 1, stride=1, stride_axis=0)[:, taps:]
        sums.append(jnp.sum(lags, axis=0, keepdims=True))
    return jnp.concatenate(sums, axis=0)


def inner_scores_kernel(taps, group_width, half, q_ref, og_ref, k_ref, v_ref, out_ref):
    begin = half * og_ref.shape[1]
    for own, rows in tiles(og_ref.shape[1], group_width):
        c = slice(begin + own.start, begin + own.stop)
        grad_mix = widen(og_ref[taps:, own]) * widen(q_ref[taps:, c])
        out_ref[rows, :] = lag_sums(taps, group_width, grad_mix, product(k_ref[:, c], v_ref[:, c]))


def scores_kernel(taps, group_width, q_ref, *refs):
    og_refs, (k_ref, v_ref, early_ref, inner_ref, out_ref) = refs[:HALVES], refs[HALVES:]
    for c, rows in tiles(k_ref.shape[1], group_width):
        there = c.stop <= og_refs[0].shape[1]
        last = taps if there else k_ref.shape[0]
        grad_mix = widen(columns_of(og_refs, c)[:last]) * widen(q_ref[:last, c])
        window = product(k_ref[:last, c], v_ref[:last, c])
        window = jnp.concatenate([early_ref[:, c], window], axis=0)
        sums = lag_sums(taps, group_width, grad_mix, window)
        sums = sums + inner_ref[rows, :] if there else sums
        out_ref[rows, :] = sums.astype(out_ref.dtype)


def turned_base(filter_ref):
    taps = filter_ref.shape[1]
    tap = lax.broadcasted_iota(jnp.int32, (taps, 2 * taps), 0)
    place = lax.broadcasted_iota(jnp.int32, (taps, 2 * taps), 1)
    turn = (tap + place == taps).astype(jnp.bfloat16)
    return jnp.dot(filter_ref[...].astype(jnp.bfloat16), turn, preferred_element_type=jnp.float32)


def inner_mixed_kernel(taps, group_width, k_ref, v_ref, filter_ref, out_ref):
    blocks = (k_ref.shape[0] - taps) // BLOCK
    base = turned_base(filter_ref)
    for c, rows in tiles(k_ref.shape[1], group_width):
        window = product(k_ref[:, c], v_ref[:, c])
        out_ref[:, c] = convolved(base[rows], window, blocks, taps, group_width)


def mixed_kernel(taps, group_width, k_ref, v_ref, early_ref, filter_ref, inner_ref, *refs):
    og_refs, out_ref = refs[:HALVES], refs[HALVES]
    blocks = taps // BLOCK
    base = turned_base(filter_ref)
    for c, rows in tiles(k_ref.shape[1], group_width):
        window = product(k_ref[:taps, c], v_ref[:taps, c])
        window = jnp.concatenate([early_ref[:, c], window], axis=0)
        mixed = convolved(base[rows], window, blocks, taps, group_width)
        og = columns_of(og_refs, c)
        out_ref[:taps, c] = (widen(og[:taps]) * mixed).astype(jnp.bfloat16)
        out_ref[taps:, c] = (widen(og[taps:]) * inner_ref[:, c]).astype(jnp.bfloat16)


def back_columns(taps, group_width, half, rows, q_ref, k_ref, v_ref, filter_ref, og_ref, late_ref):
    blocks = (rows.stop - rows.start) // BLOCK
    coeffs = widen(filter_ref[...].astype(jnp.bfloat16))
    base = jnp.concatenate([coeffs, jnp.zeros_like(coeffs)], axis=1)
    begin = half * og_ref.shape[1]
    last = min(rows.stop + taps, og_ref.shape[0])
    for own, _ in tiles(og_ref.shape[1], group_width):
        c = slice(begin + own.start, begin + own.stop)
        groups = slice(c.start // group_width, c.stop // group_width)
        window = product(og_ref[rows.start : last, own], q_ref[rows.start : last, c])
        if last < rows.stop + taps:
            window = jnp.concatenate([window, late_ref[:, own]], axis=0)
        back = convolved(base[groups], window, blocks, taps, group_width)
        yield own, [(back * widen(ref[rows, c])).astype(jnp.bfloat16) for ref in (v_ref, k_ref)]


def first_back_kernel(taps, group_width, *refs):
    sides, (og_ref, other_ref, late_ref, qg_ref), refs = refs[:4], refs[4:8], refs[8:]
    kg_ref, vg_ref, kg_top, vg_top, out_ref, sem = refs
    copy = pltpu.make_async_copy(qg_ref, out_ref, sem)
    copy.start()
    height = og_ref.shape[0]
    for own, (kg, vg) in back_columns(taps, group_width, 0, slice(0, height), *sides, og_ref, late_ref):
        kg_ref[:, own] = kg
        vg_ref[:, own] = vg
    above = slice(0, kg_top.shape[0])
    for own, (kg, vg) in back_columns(taps, group_width, 1, above, *sides, other_ref, None):
        kg_top[:, own] = kg
        vg_top[:, own] = vg
    copy.wait()


def second_back_kernel(taps, group_width, *refs):
    inputs, done_refs, refs = refs[:6], refs[6:10], refs[10:]
    kg_ref, vg_ref, k_stage, v_stage, first_sem, k_sem, v_sem = refs
    width = done_refs[0].shape[1]
    height = done_refs[2].shape[0]
    copies = []
    for n, (done_ref, out_ref) in enumerate(zip(done_refs, (kg_ref, vg_ref, kg_ref, vg_ref))):
        place = (pl.ds(0, done_ref.shape[0]), pl.ds(0 if n < 2 else width, done_ref.shape[1]))
        copies.append(pltpu.make_async_copy(done_ref, out_ref.at[place], first_sem.at[n]))
    for copy in copies:
        copy.start()
    rows = slice(height, kg_ref.shape[0])
    for own, (kg, vg) in back_columns(taps, group_width, 1, rows, *inputs):
        k_stage[:, own] = kg
        v_stage[:, own] = vg
        copies += send_out(k_stage, kg_ref, k_sem, own, height, width)
        copies += send_out(v_stage, vg_ref, v_sem, own, height, width)
    for copy in copies:
        copy.wait()


def call(kernel, name, args, outs, cost, in_hbm_from=None, scratch=()):
    kept = len(outs) if in_hbm_from is None else in_hbm_from
    return pl.pallas_call(
        kernel,
        in_specs=[VMEM] * len(args),
        out_specs=[VMEM] * kept + [ANYWHERE] * (len(outs) - kept),
        out_shape=outs,
        scratch_shapes=scratch,
        name=name,
        cost_estimate=pl.CostEstimate(flops=cost, bytes_accessed=1000, transcendentals=0),
        compiler_params=pltpu.CompilerParams(vmem_limit_bytes=LIMIT * 1024 * 1024),
    )(*args)


def local(queries, keys, values, out_grad, filters):
    q, k, v = queries[0], keys[0], values[0]
    rows, channels = q.shape
    groups, taps = filters.shape
    group_width = channels // groups
    wide = jax.ShapeDtypeStruct((rows, channels), jnp.bfloat16)
    edge = jax.ShapeDtypeStruct((taps, channels), jnp.bfloat16)
    small = jax.ShapeDtypeStruct((groups, taps), jnp.float32)
    half_small = jax.ShapeDtypeStruct((groups // HALVES, taps), jnp.float32)
    thin = jax.ShapeDtypeStruct((groups, taps), TRAVEL)
    width = channels // HALVES
    count = lax.axis_size("tp")
    height = rows // count
    far = count - NEAR
    piece = jax.ShapeDtypeStruct((height, channels), jnp.bfloat16)
    half_piece = jax.ShapeDtypeStruct((height, width), jnp.bfloat16)
    first_cuts = [(step, -1) for step in range(1, NEAR)] + [(step, 0) for step in range(NEAR, count)]
    second_cuts = [(0, -1)] + [(step, 1) for step in range(NEAR, count)]
    pieces = [half_piece if half >= 0 else piece for _, half in first_cuts]
    second_pieces = [half_piece if half >= 0 else piece for _, half in second_cuts]
    half_wide = jax.ShapeDtypeStruct((rows, width), jnp.bfloat16)
    half_edge = jax.ShapeDtypeStruct((taps, width), jnp.bfloat16)
    *parts, tail = pl.pallas_call(
        functools.partial(pack_kernel, first_cuts, count, lax.axis_size("ctx") - 1),
        in_specs=[ANYWHERE] * 3,
        out_specs=[ANYWHERE] * len(pieces) + [VMEM],
        out_shape=pieces + [edge],
        scratch_shapes=[pltpu.VMEM(edge.shape, edge.dtype)] * 2
        + [pltpu.SemaphoreType.DMA((len(pieces),)), pltpu.SemaphoreType.DMA((2,))],
        name="pack",
        compiler_params=pltpu.CompilerParams(vmem_limit_bytes=LIMIT * 1024 * 1024),
    )(*[in_hbm(a) for a in (out_grad[0], k, v)])
    early = passed_round(tail, "ctx", 1)
    near = [exchanged(part, "tp", step) for step, part in enumerate(parts[: NEAR - 1], 1)]
    grad_in, near[-1] = lax.optimization_barrier((out_grad[0], near[-1]))
    own, *second_parts = pl.pallas_call(
        functools.partial(second_pack_kernel, second_cuts, count),
        in_specs=[ANYWHERE],
        out_specs=[ANYWHERE] * len(second_pieces),
        out_shape=second_pieces,
        scratch_shapes=[pltpu.SemaphoreType.DMA((len(second_pieces),))],
        name="second_pack",
        compiler_params=pltpu.CompilerParams(vmem_limit_bytes=LIMIT * 1024 * 1024),
    )(in_hbm(grad_in))
    near = [own] + near
    inner_rows = jax.ShapeDtypeStruct((rows - taps, channels), jnp.float32)
    (inner,) = call(
        functools.partial(inner_mixed_kernel, taps, group_width), "inner_causal", (k, v, filters), [inner_rows], COST
    )
    grads, heads, inners = [], [], []
    for half in range(HALVES):
        mine = second_parts if half else parts[NEAR - 1 :]
        brought_in = [exchanged(part, "tp", step) for step, part in enumerate(mine, NEAR)]
        if half:
            brought_in, inners[0] = lax.optimization_barrier((brought_in, inners[0]))
        else:
            brought_in, inner = lax.optimization_barrier((brought_in, inner))
        if height % 16 == 0:
            grad, head = call(
                functools.partial(gather_kernel, count, half), "gather", (q, *near, *brought_in),
                [half_wide, half_edge], 1000,
            )
        else:
            here = lax.axis_index("tp")
            c = slice(half * width, (half + 1) * width)
            grad = jnp.zeros(half_wide.shape, half_wide.dtype)
            for step, part in enumerate([part[:, c] for part in near] + brought_in):
                place = partner(here, step, count)
                grad = lax.dynamic_update_slice_in_dim(grad, part, place * height, 0)
            head = product(grad[:taps], q[:taps, c])
        grads.append(grad)
        heads.append(head)
        if not half:
            (lags,) = call(
                functools.partial(inner_scores_kernel, taps, group_width, 0), "inner_scores", (q, grad, k, v), [half_small], COST
            )
            inners.append(lags)
    work = functools.partial
    (lags,) = call(
        work(scores_kernel, taps, group_width), "edge_scores", (q, *grads, k, v, early, *inners), [thin], COST
    )
    lates = [passed_along(head, "ctx", -1) for head in heads]
    (query_grad,) = call(
        work(mixed_kernel, taps, group_width), "causal", (k, v, early, filters, inner, *grads), [wide], COST
    )
    lags, query_grad = first_rounds(lags, query_grad)
    sides = (q, k, v, filters)
    kept, above, rest = [
        jax.ShapeDtypeStruct((size, width), jnp.bfloat16) for size in (rows, rows - taps, taps)
    ]
    *done, query_grad = call(
        work(first_back_kernel, taps, group_width), "adjoint", (*sides, *grads, lates[0], query_grad),
        [kept, kept, above, above, wide], COST_A, 4, [pltpu.SemaphoreType.DMA],
    )
    steps = pltpu.SemaphoreType.DMA((-(-width // STEP),))
    key_grad, value_grad = call(
        work(second_back_kernel, taps, group_width), "adjoint",
        (*sides, grads[1], lates[1], *done), [wide, wide], COST_B, 0,
        [pltpu.VMEM(rest.shape, rest.dtype)] * 2 + [pltpu.SemaphoreType.DMA((4,)), steps, steps],
    )
    lags, key_grad = last_round(lags, key_grad)
    scale = 1.0 / math.sqrt(lax.axis_size("dp") * lax.axis_size("ctx") * rows * group_width)
    return (query_grad[None], key_grad[None], value_grad[None], jnp.flip(lags, 1) * scale)


COST = 100_000_000
COST_A = 1_000_000_000
COST_B = 1000
HALVES = 2
NEAR = 2
TRAVEL = jnp.bfloat16
LIMIT = 8


def solution(mesh):
    in_specs = (
        P("dp", "ctx", "tp"),
        P("dp", "ctx", "tp"),
        P("dp", "ctx", "tp"),
        P("dp", ("ctx", "tp"), None),
        P("tp", None),
    )
    out_specs = (P("dp", "ctx", "tp"), P("dp", "ctx", "tp"), P("dp", "ctx", "tp"), P("tp", None))
    return jax.shard_map(local, mesh=mesh, in_specs=in_specs, out_specs=out_specs, check_vma=False)
```

```python
import functools
import math

import jax
import jax.numpy as jnp
from jax import lax
from jax.experimental import pallas as pl
from jax.experimental.pallas import tpu as pltpu
from jax.sharding import PartitionSpec as P

LANES = 128
BLOCK = 32
STEP = 1 * LANES
VMEM = pl.BlockSpec(memory_space=pltpu.VMEM)
ANYWHERE = pl.BlockSpec(memory_space=pl.ANY)


def in_hbm(value):
    return pltpu.with_memory_space_constraint(value, pltpu.HBM)


def widen(value):
    return value.astype(jnp.float32)


def product(left, right):
    return (widen(left) * widen(right)).astype(jnp.bfloat16)


def passed_along(value, axis, steps):
    count = lax.axis_size(axis)
    first, last = (max(0, -steps), min(count, count - steps))
    return lax.ppermute(value, axis, [(source, source + steps) for source in range(first, last)])


def passed_round(value, axis, steps):
    count = lax.axis_size(axis)
    return lax.ppermute(value, axis, [(index, (index + steps) % count) for index in range(count)])


def partner(index, step, count):
    if count & (count - 1) == 0:
        return index ^ step
    return (index - step + count) % count


def target(index, step, count):
    if count & (count - 1) == 0:
        return index ^ step
    return (index + step) % count


def exchanged(part, axis, step):
    count = lax.axis_size(axis)
    pairs = [(index, target(index, step, count)) for index in range(count)]
    return lax.ppermute(part, axis, pairs)


def add_kernel(*refs):
    *parts, out_ref = refs
    total = [widen(part[...]) for part in parts]
    while len(total) > 1:
        total = [sum(total[n : n + 2][1:], total[n]) for n in range(0, len(total), 2)]
    out_ref[...] = total[0].astype(out_ref.dtype)


def added(parts, dtype):
    return pl.pallas_call(
        add_kernel,
        in_specs=[VMEM] * len(parts),
        out_specs=VMEM,
        out_shape=jax.ShapeDtypeStruct(parts[0].shape, dtype),
        name="add",
        compiler_params=pltpu.CompilerParams(vmem_limit_bytes=LIMIT * 1024 * 1024),
    )(*parts)


def brought(value, step):
    axes = ("ctx", "dp")
    count = lax.axis_size("ctx") * lax.axis_size("dp")
    return lax.ppermute(value, axes, [(index, index ^ step) for index in range(count)])


def rounds_of_sum():
    rounds, base = [], 1
    for size in (lax.axis_size("dp"), lax.axis_size("ctx")):
        if size & (size - 1):
            return None
        while size > 1:
            width = 4 if size % 4 == 0 else 2
            rounds.append([base * step for step in range(1, width)])
            base *= width
            size //= width
    return rounds


def first_rounds(value, after):
    rounds = rounds_of_sum()
    if rounds is None:
        return lax.psum(widen(value), ("dp", "ctx")), after
    for n, steps in enumerate(rounds[:-1]):
        parts = [value] + [brought(value, step) for step in steps]
        if n == 0:
            parts, after = lax.optimization_barrier((parts, after))
        value = added(parts, TRAVEL if n == len(rounds) - 2 else jnp.float32)
    return value, after


def last_round(value, after):
    rounds = rounds_of_sum()
    if not rounds:
        return [widen(value)], after
    parts = [value] + [brought(value, step) for step in rounds[-1]]
    parts, after = lax.optimization_barrier((parts, after))
    return parts, after


def finish_kernel(scale, *refs):
    parts, (out_ref, stage_ref, sem) = refs[:-3], refs[-3:]
    total = [widen(part[...]) for part in parts]
    while len(total) > 1:
        total = [total[m] + total[m + 1] for m in range(0, len(total), 2)]
    size = total[0].shape[1]
    backward = size - 1 - lax.broadcasted_iota(jnp.int32, total[0].shape, 1)
    turned = jnp.take_along_axis(total[0], backward, axis=1, mode="promise_in_bounds")
    stage_ref[...] = turned * scale
    copy = pltpu.make_async_copy(stage_ref, out_ref, sem)
    copy.start()
    copy.wait()


def windows(rows, blocks, height):
    return jnp.concatenate([rows[BLOCK * b : BLOCK * b + height] for b in range(blocks)], axis=1)


def bands(base, count, width):
    rows = []
    for group in range(count):
        row = jnp.broadcast_to(base[group : group + 1, :], (BLOCK, base.shape[1]))
        row = pltpu.roll(row, 0, 1, stride=1, stride_axis=0)
        rows.append(row[:, :width].astype(jnp.bfloat16))
    return jnp.concatenate(rows, axis=0)


def convolved(base, window, blocks, taps, group_width):
    count = LANES // group_width
    every = jnp.dot(
        bands(base, count, taps + BLOCK),
        windows(window, blocks, taps + BLOCK),
        preferred_element_type=jnp.float32,
    )
    lane_group = lax.broadcasted_iota(jnp.int32, (BLOCK, LANES), 1) // group_width
    outs = []
    for b in range(blocks):
        columns = slice(b * LANES, (b + 1) * LANES)
        out = every[:BLOCK, columns]
        for group in range(1, count):
            out = jnp.where(
                lane_group == group, every[group * BLOCK : (group + 1) * BLOCK, columns], out
            )
        outs.append(out)
    return jnp.concatenate(outs, axis=0)


def tiles(channels, group_width):
    count = LANES // group_width
    for tile in range(channels // LANES):
        yield slice(tile * LANES, (tile + 1) * LANES), slice(tile * count, (tile + 1) * count)


def send_out(stage_ref, out_ref, sem, c, below, right):
    if c.stop % STEP == 0 or c.stop == stage_ref.shape[1]:
        begin = (c.stop - 1) // STEP * STEP
        place = (pl.ds(below, stage_ref.shape[0]), pl.ds(right + begin, c.stop - begin))
        copy = pltpu.make_async_copy(
            stage_ref.at[:, pl.ds(begin, c.stop - begin)], out_ref.at[place], sem.at[begin // STEP]
        )
        copy.start()
        return [copy]
    return []


def cut_out(cuts_of, count, grad_ref, parts, sem):
    here = lax.axis_index("tp")
    width = grad_ref.shape[1] // count
    cuts = []
    for n, ((step, half), part) in enumerate(zip(cuts_of, parts)):
        columns = part.shape[1]
        place = pl.multiple_of(target(here, step, count) * width + max(half, 0) * columns, columns)
        cuts.append(pltpu.make_async_copy(grad_ref.at[:, pl.ds(place, columns)], part, sem.at[n]))
    return cuts


def second_pack_kernel(cuts_of, count, grad_ref, *refs):
    cuts = cut_out(cuts_of, count, grad_ref, refs[:-1], refs[-1])
    for copy in cuts:
        copy.start()
    for copy in cuts:
        copy.wait()


def pack_kernel(cuts_of, count, last, grad_ref, k_ref, v_ref, *refs):
    parts, (tail_ref, k_stage, v_stage, part_sem, tail_sem) = refs[:-5], refs[-5:]
    height = k_stage.shape[0]
    below = pl.ds(k_ref.shape[0] - height, height)
    tails = [
        pltpu.make_async_copy(ref.at[below], into, tail_sem.at[n])
        for n, (ref, into) in enumerate([(k_ref, k_stage), (v_ref, v_stage)])
    ]
    cuts = cut_out(cuts_of, count, grad_ref, parts, part_sem)
    for copy in tails + cuts:
        copy.start()
    for copy in tails:
        copy.wait()
    place = lax.axis_index("ctx")

    @pl.when(place == last)
    def _():
        tail_ref[...] = jnp.zeros(tail_ref.shape, tail_ref.dtype)

    @pl.when(place != last)
    def _():
        tail_ref[...] = product(k_stage[...], v_stage[...])

    for copy in cuts:
        copy.wait()


def gather_kernel(count, half, q_ref, *refs):
    parts, (og_ref, head_ref) = refs[:-2], refs[-2:]
    height, width = parts[-1].shape
    here = lax.axis_index("tp")
    head = head_ref.shape[0]
    c = slice(half * width, (half + 1) * width)
    for step, part in enumerate(parts):
        place = partner(here, step, count)
        rows = pl.ds(pl.multiple_of(place * height, height), height)
        og_ref[rows, :] = part[:, c] if step < NEAR else part[...]
    head_ref[...] = product(og_ref[:head, :], q_ref[:head, c])


def columns_of(refs, c):
    width = refs[0].shape[1]
    half = c.start // width
    return refs[half][:, c.start - half * width : c.stop - half * width]


def lag_sums(taps, group_width, grad_mix, window):
    blocks = grad_mix.shape[0] // BLOCK
    count = LANES // group_width
    upward = 7 - lax.broadcasted_iota(jnp.int32, (8, LANES), 0)
    lane = lax.broadcasted_iota(jnp.int32, (BLOCK, blocks * LANES), 1)
    lane_group = (lane % LANES) // group_width
    turned = []
    for b in range(blocks):
        for end in range((b + 1) * BLOCK, b * BLOCK, -8):
            eight = grad_mix[end - 8 : end]
            turned.append(jnp.take_along_axis(eight, upward, axis=0, mode="promise_in_bounds"))
    own = windows(jnp.concatenate(turned, axis=0).astype(jnp.bfloat16), blocks, BLOCK)
    split = [jnp.where(lane_group == g, own, jnp.zeros_like(own)) for g in range(count)]
    scores = lax.dot_general(
        jnp.concatenate(split, axis=0),
        windows(window, blocks, taps + BLOCK),
        (((1,), (1,)), ((), ())),
        preferred_element_type=jnp.float32,
    )
    spare = jnp.zeros((scores.shape[0], 2 * taps - scores.shape[1]), jnp.float32)
    scores = jnp.concatenate([scores, spare], axis=1)
    sums = []
    for g in range(count):
        lags = scores[g * BLOCK : (g + 1) * BLOCK]
        lags = pltpu.roll(lags, taps - BLOCK, 1, stride=1, stride_axis=0)[:, taps:]
        sums.append(jnp.sum(lags, axis=0, keepdims=True))
    return jnp.concatenate(sums, axis=0)


def inner_scores_kernel(taps, group_width, half, q_ref, og_ref, k_ref, v_ref, out_ref):
    begin = half * og_ref.shape[1]
    for own, rows in tiles(og_ref.shape[1], group_width):
        c = slice(begin + own.start, begin + own.stop)
        grad_mix = widen(og_ref[taps:, own]) * widen(q_ref[taps:, c])
        out_ref[rows, :] = lag_sums(taps, group_width, grad_mix, product(k_ref[:, c], v_ref[:, c]))


def scores_kernel(taps, group_width, q_ref, *refs):
    og_refs, (k_ref, v_ref, early_ref, inner_ref, out_ref) = refs[:HALVES], refs[HALVES:]
    for c, rows in tiles(k_ref.shape[1], group_width):
        there = c.stop <= og_refs[0].shape[1]
        last = taps if there else k_ref.shape[0]
        grad_mix = widen(columns_of(og_refs, c)[:last]) * widen(q_ref[:last, c])
        window = product(k_ref[:last, c], v_ref[:last, c])
        window = jnp.concatenate([early_ref[:, c], window], axis=0)
        sums = lag_sums(taps, group_width, grad_mix, window)
        sums = sums + inner_ref[rows, :] if there else sums
        out_ref[rows, :] = sums.astype(out_ref.dtype)


def turned_base(filter_ref):
    taps = filter_ref.shape[1]
    tap = lax.broadcasted_iota(jnp.int32, (taps, 2 * taps), 0)
    place = lax.broadcasted_iota(jnp.int32, (taps, 2 * taps), 1)
    turn = (tap + place == taps).astype(jnp.bfloat16)
    return jnp.dot(filter_ref[...].astype(jnp.bfloat16), turn, preferred_element_type=jnp.float32)


def inner_mixed_kernel(taps, group_width, k_ref, v_ref, filter_ref, out_ref):
    blocks = (k_ref.shape[0] - taps) // BLOCK
    base = turned_base(filter_ref)
    for c, rows in tiles(k_ref.shape[1], group_width):
        window = product(k_ref[:, c], v_ref[:, c])
        out_ref[:, c] = convolved(base[rows], window, blocks, taps, group_width)


def mixed_kernel(taps, group_width, k_ref, v_ref, early_ref, filter_ref, inner_ref, *refs):
    og_refs, out_ref = refs[:HALVES], refs[HALVES]
    blocks = taps // BLOCK
    base = turned_base(filter_ref)
    for c, rows in tiles(k_ref.shape[1], group_width):
        window = product(k_ref[:taps, c], v_ref[:taps, c])
        window = jnp.concatenate([early_ref[:, c], window], axis=0)
        mixed = convolved(base[rows], window, blocks, taps, group_width)
        og = columns_of(og_refs, c)
        out_ref[:taps, c] = (widen(og[:taps]) * mixed).astype(jnp.bfloat16)
        out_ref[taps:, c] = (widen(og[taps:]) * inner_ref[:, c]).astype(jnp.bfloat16)


def back_columns(taps, group_width, half, rows, q_ref, k_ref, v_ref, filter_ref, og_ref, late_ref):
    blocks = (rows.stop - rows.start) // BLOCK
    coeffs = widen(filter_ref[...].astype(jnp.bfloat16))
    base = jnp.concatenate([coeffs, jnp.zeros_like(coeffs)], axis=1)
    begin = half * og_ref.shape[1]
    last = min(rows.stop + taps, og_ref.shape[0])
    for own, _ in tiles(og_ref.shape[1], group_width):
        c = slice(begin + own.start, begin + own.stop)
        groups = slice(c.start // group_width, c.stop // group_width)
        window = product(og_ref[rows.start : last, own], q_ref[rows.start : last, c])
        if last < rows.stop + taps:
            window = jnp.concatenate([window, late_ref[:, own]], axis=0)
        back = convolved(base[groups], window, blocks, taps, group_width)
        yield own, [(back * widen(ref[rows, c])).astype(jnp.bfloat16) for ref in (v_ref, k_ref)]


def first_back_kernel(taps, group_width, *refs):
    sides, (og_ref, other_ref, late_ref, qg_ref), refs = refs[:4], refs[4:8], refs[8:]
    kg_ref, vg_ref, kg_top, vg_top, out_ref, sem = refs
    copy = pltpu.make_async_copy(qg_ref, out_ref, sem)
    copy.start()
    height = og_ref.shape[0]
    for own, (kg, vg) in back_columns(taps, group_width, 0, slice(0, height), *sides, og_ref, late_ref):
        kg_ref[:, own] = kg
        vg_ref[:, own] = vg
    above = slice(0, kg_top.shape[0])
    for own, (kg, vg) in back_columns(taps, group_width, 1, above, *sides, other_ref, None):
        kg_top[:, own] = kg
        vg_top[:, own] = vg
    copy.wait()


def second_back_kernel(taps, group_width, *refs):
    inputs, done_refs, refs = refs[:6], refs[6:10], refs[10:]
    kg_ref, vg_ref, k_stage, v_stage, first_sem, k_sem, v_sem = refs
    width = done_refs[0].shape[1]
    height = done_refs[2].shape[0]
    copies = []
    for n, (done_ref, out_ref) in enumerate(zip(done_refs, (kg_ref, vg_ref, kg_ref, vg_ref))):
        place = (pl.ds(0, done_ref.shape[0]), pl.ds(0 if n < 2 else width, done_ref.shape[1]))
        copies.append(pltpu.make_async_copy(done_ref, out_ref.at[place], first_sem.at[n]))
    for copy in copies:
        copy.start()
    rows = slice(height, kg_ref.shape[0])
    for own, (kg, vg) in back_columns(taps, group_width, 1, rows, *inputs):
        k_stage[:, own] = kg
        v_stage[:, own] = vg
        copies += send_out(k_stage, kg_ref, k_sem, own, height, width)
        copies += send_out(v_stage, vg_ref, v_sem, own, height, width)
    for copy in copies:
        copy.wait()


def call(kernel, name, args, outs, cost, in_hbm_from=None, scratch=()):
    kept = len(outs) if in_hbm_from is None else in_hbm_from
    return pl.pallas_call(
        kernel,
        in_specs=[VMEM] * len(args),
        out_specs=[VMEM] * kept + [ANYWHERE] * (len(outs) - kept),
        out_shape=outs,
        scratch_shapes=scratch,
        name=name,
        cost_estimate=pl.CostEstimate(flops=cost, bytes_accessed=1000, transcendentals=0),
        compiler_params=pltpu.CompilerParams(vmem_limit_bytes=LIMIT * 1024 * 1024),
    )(*args)


def local(queries, keys, values, out_grad, filters):
    q, k, v = queries[0], keys[0], values[0]
    rows, channels = q.shape
    groups, taps = filters.shape
    group_width = channels // groups
    wide = jax.ShapeDtypeStruct((rows, channels), jnp.bfloat16)
    edge = jax.ShapeDtypeStruct((taps, channels), jnp.bfloat16)
    small = jax.ShapeDtypeStruct((groups, taps), jnp.float32)
    half_small = jax.ShapeDtypeStruct((groups // HALVES, taps), jnp.float32)
    thin = jax.ShapeDtypeStruct((groups, taps), TRAVEL)
    width = channels // HALVES
    count = lax.axis_size("tp")
    height = rows // count
    far = count - NEAR
    piece = jax.ShapeDtypeStruct((height, channels), jnp.bfloat16)
    half_piece = jax.ShapeDtypeStruct((height, width), jnp.bfloat16)
    first_cuts = [(step, -1) for step in range(1, NEAR)] + [(step, 0) for step in range(NEAR, count)]
    second_cuts = [(0, -1)] + [(step, 1) for step in range(NEAR, count)]
    pieces = [half_piece if half >= 0 else piece for _, half in first_cuts]
    second_pieces = [half_piece if half >= 0 else piece for _, half in second_cuts]
    half_wide = jax.ShapeDtypeStruct((rows, width), jnp.bfloat16)
    half_edge = jax.ShapeDtypeStruct((taps, width), jnp.bfloat16)
    *parts, tail = pl.pallas_call(
        functools.partial(pack_kernel, first_cuts, count, lax.axis_size("ctx") - 1),
        in_specs=[ANYWHERE] * 3,
        out_specs=[ANYWHERE] * len(pieces) + [VMEM],
        out_shape=pieces + [edge],
        scratch_shapes=[pltpu.VMEM(edge.shape, edge.dtype)] * 2
        + [pltpu.SemaphoreType.DMA((len(pieces),)), pltpu.SemaphoreType.DMA((2,))],
        name="pack",
        compiler_params=pltpu.CompilerParams(vmem_limit_bytes=LIMIT * 1024 * 1024),
    )(*[in_hbm(a) for a in (out_grad[0], k, v)])
    early = passed_round(tail, "ctx", 1)
    near = [exchanged(part, "tp", step) for step, part in enumerate(parts[: NEAR - 1], 1)]
    grad_in, near[-1] = lax.optimization_barrier((out_grad[0], near[-1]))
    own, *second_parts = pl.pallas_call(
        functools.partial(second_pack_kernel, second_cuts, count),
        in_specs=[ANYWHERE],
        out_specs=[ANYWHERE] * len(second_pieces),
        out_shape=second_pieces,
        scratch_shapes=[pltpu.SemaphoreType.DMA((len(second_pieces),))],
        name="second_pack",
        compiler_params=pltpu.CompilerParams(vmem_limit_bytes=LIMIT * 1024 * 1024),
    )(in_hbm(grad_in))
    near = [own] + near
    inner_rows = jax.ShapeDtypeStruct((rows - taps, channels), jnp.float32)
    (inner,) = call(
        functools.partial(inner_mixed_kernel, taps, group_width), "inner_causal", (k, v, filters), [inner_rows], COST
    )
    grads, heads, inners = [], [], []
    for half in range(HALVES):
        mine = second_parts if half else parts[NEAR - 1 :]
        brought_in = [exchanged(part, "tp", step) for step, part in enumerate(mine, NEAR)]
        if half:
            brought_in, inners[0] = lax.optimization_barrier((brought_in, inners[0]))
        else:
            brought_in, inner = lax.optimization_barrier((brought_in, inner))
        if height % 16 == 0:
            grad, head = call(
                functools.partial(gather_kernel, count, half), "gather", (q, *near, *brought_in),
                [half_wide, half_edge], 1000,
            )
        else:
            here = lax.axis_index("tp")
            c = slice(half * width, (half + 1) * width)
            grad = jnp.zeros(half_wide.shape, half_wide.dtype)
            for step, part in enumerate([part[:, c] for part in near] + brought_in):
                place = partner(here, step, count)
                grad = lax.dynamic_update_slice_in_dim(grad, part, place * height, 0)
            head = product(grad[:taps], q[:taps, c])
        grads.append(grad)
        heads.append(head)
        if not half:
            (lags,) = call(
                functools.partial(inner_scores_kernel, taps, group_width, 0), "inner_scores", (q, grad, k, v), [half_small], COST
            )
            inners.append(lags)
    work = functools.partial
    (lags,) = call(
        work(scores_kernel, taps, group_width), "edge_scores", (q, *grads, k, v, early, *inners), [thin], COST
    )
    lates = [passed_along(head, "ctx", -1) for head in heads]
    (query_grad,) = call(
        work(mixed_kernel, taps, group_width), "causal", (k, v, early, filters, inner, *grads), [wide], COST
    )
    lags, query_grad = first_rounds(lags, query_grad)
    sides = (q, k, v, filters)
    kept, above, rest = [
        jax.ShapeDtypeStruct((size, width), jnp.bfloat16) for size in (rows, rows - taps, taps)
    ]
    *done, query_grad = call(
        work(first_back_kernel, taps, group_width), "adjoint", (*sides, *grads, lates[0], query_grad),
        [kept, kept, above, above, wide], COST_A, 4, [pltpu.SemaphoreType.DMA],
    )
    steps = pltpu.SemaphoreType.DMA((-(-width // STEP),))
    key_grad, value_grad = call(
        work(second_back_kernel, taps, group_width), "adjoint",
        (*sides, grads[1], lates[1], *done), [wide, wide], COST_B, 0,
        [pltpu.VMEM(rest.shape, rest.dtype)] * 2 + [pltpu.SemaphoreType.DMA((4,)), steps, steps],
    )
    lags, key_grad = last_round(lags, key_grad)
    scale = 1.0 / math.sqrt(lax.axis_size("dp") * lax.axis_size("ctx") * rows * group_width)
    (filter_grad,) = call(
        work(finish_kernel, scale), "finish", lags, [small], COST_B, 0,
        [pltpu.VMEM(small.shape, small.dtype), pltpu.SemaphoreType.DMA],
    )
    return (query_grad[None], key_grad[None], value_grad[None], filter_grad)


COST = 100_000_000
COST_A = 1_000_000_000
COST_B = 1000
HALVES = 2
NEAR = 2
TRAVEL = jnp.bfloat16
LIMIT = 8


def solution(mesh):
    in_specs = (
        P("dp", "ctx", "tp"),
        P("dp", "ctx", "tp"),
        P("dp", "ctx", "tp"),
        P("dp", ("ctx", "tp"), None),
        P("tp", None),
    )
    out_specs = (P("dp", "ctx", "tp"), P("dp", "ctx", "tp"), P("dp", "ctx", "tp"), P("tp", None))
    return jax.shard_map(local, mesh=mesh, in_specs=in_specs, out_specs=out_specs, check_vma=False)
```
